512 devices in a mesh: section: 8 (over y, z_hi), tp: 64 (over z_lo, x, core).
Axes of the slice: x: 4, y: 4, z: 16 (z_hi: 2, z_lo: 8; z = z_hi * 8 + z_lo), core: 2. Of those that a mesh axis runs over, the one named last changes fastest.
Arguments:
- acts: bfloat16 [8192, 4096], P(('section', 'tp')), may hold values from -6 to 6
- cotangent: bfloat16 [8192, 4096], P(('section', 'tp')), may hold values from -6 to 6
- gains: float32 [8, 2, 4096], P('section'), may hold values from 0.1 to 1.9
- gate_blocks: bfloat16 [8, 192, 128, 128], P('section', 'tp'), may hold values from -0.4375 to 0.4375
- up_blocks: bfloat16 [8, 192, 128, 128], P('section', 'tp'), may hold values from -0.4375 to 0.4375
- down_blocks: bfloat16 [8, 192, 128, 128], P('section', 'tp'), may hold values from -0.21875 to 0.21875
- block_place: int32 [8, 192], P('section'), may hold values from -1 to 63, as said below
Outputs:
- layer_out: bfloat16 [8192, 4096], P(('section', 'tp'))
- grad_back: bfloat16 [8192, 4096], P(('section', 'tp'))
- gate_grad: bfloat16 [8, 192, 128, 128], P('section', 'tp')
- up_grad: bfloat16 [8, 192, 128, 128], P('section', 'tp')
- down_grad: bfloat16 [8, 192, 128, 128], P('section', 'tp')
- gain_grad: float32 [8, 2, 4096], P('section')
The draws below stay inside these ranges and needn't reach their ends.
Inputs may be any that keep to these rules, and one draw needn't show every extreme that they name: `block_place`: A value p >= 0 places the slot at feature block p // 2 and at block p % 2 of its device's hidden units; -1 marks an empty slot. Slots j with the same j // 3 belong to one device; on one device the live slots come first and their values are distinct; every device has 1 or more live slots, and one device of every section has all 3 live.
All inputs are finite; a program needn't handle non-finite values.
Results may differ from the reference program's by a relative error of at most 0.0073.
Values may be sent and summed in bfloat16 or wider, within the bound.
No kernel may reach another device: no remote copies, remote signals or barrier semaphores. Data moves between devices by JAX's collectives and lax.ppermute only.
A program may use at most 64 MiB of HBM per device.

```python
import jax
import jax.numpy as jnp
from jax import lax

D = 4096
BLK = 128
COLS_DEV = 2
SLOTS = 3
TOKENS = 1024
N_SECTION = 8
N_TP = 64


def draw_block_place(key, part):
    key = jax.random.fold_in(key, 7)
    count_key, full_key, order_key = jax.random.split(key, 3)
    device_count = N_SECTION * N_TP
    positions = D // BLK * COLS_DEV
    counts = jax.random.randint(count_key, (N_SECTION, N_TP), SLOTS // 3, SLOTS + 1)
    fullest = jax.random.randint(full_key, (N_SECTION, 1), 0, N_TP)
    counts = jnp.where(jnp.arange(N_TP)[None, :] == fullest, SLOTS, counts)

    def one_order(subkey):
        return jax.random.permutation(subkey, positions)
    orders = jax.vmap(one_order)(jax.random.split(order_key, device_count))
    chosen = orders[:, :SLOTS].reshape(N_SECTION, N_TP, SLOTS)
    slot_index = jnp.arange(SLOTS)[None, None, :]
    placed = jnp.where(slot_index < counts[:, :, None], chosen, -1)
    return placed.reshape(N_SECTION, N_TP * SLOTS).astype(jnp.int32)


def block_scale(rng, dims, shards, low, top_value):
    factor_of, own = 1.0, jax.random.fold_in(rng, 6)
    for axis_at, shards_of in shards:
        heights = jnp.exp(jax.random.uniform(jax.random.fold_in(own, axis_at), (shards_of,), jnp.float32, low / len(shards), top_value / len(shards)))
        factor_of = factor_of * jnp.repeat(heights, dims[axis_at] // shards_of).reshape([-1 if axis == axis_at else 1 for axis in range(len(dims))])
    return factor_of


def normal_values(stream_key, shape, scale, reach, cuts=(), held_as=jnp.bfloat16):
    drawn = jax.random.normal(stream_key, shape, jnp.float32) * scale
    if len(cuts) > 0:
        drawn = block_scale(stream_key, shape, cuts, -0.22, 0.18) * drawn
    return jnp.clip(drawn, min=-reach, max=reach).astype(held_as)


def setup_inputs(seed: int = 0) -> dict:
    seeds = jax.random.split(jax.random.key(seed), 8)
    return {
        "acts": normal_values(seeds[0], (N_SECTION * TOKENS, D), 1.0, 6.0, ((0, 512),)),
        "cotangent": normal_values(seeds[1], (N_SECTION * TOKENS, D), 1.0, 6.0, ((0, 512),)),
        "gains": jnp.clip(1.0 + 0.18 * jax.random.normal(seeds[2], (N_SECTION, 2, D), jnp.float32), 0.1, 1.9),
        "gate_blocks": normal_values(seeds[3], (N_SECTION, N_TP * SLOTS, BLK, BLK), (BLK * SLOTS // COLS_DEV) ** -0.5, 0.4375, ((0, 8), (1, 64))),
        "up_blocks": normal_values(seeds[4], (N_SECTION, N_TP * SLOTS, BLK, BLK), (BLK * SLOTS // COLS_DEV) ** -0.5, 0.4375, ((0, 8), (1, 64))),
        "down_blocks": normal_values(seeds[5], (N_SECTION, N_TP * SLOTS, BLK, BLK), (BLK * SLOTS * N_TP // (D // BLK)) ** -0.5, 0.21875, ((0, 8), (1, 64))),
        "block_place": draw_block_place(jax.random.fold_in(seeds[7], 71), 0),
    }


epsilon = 1e-05
highest = lax.Precision.HIGHEST

def slot_tables(slot_place):
    live_flag = (slot_place >= 0).astype(jnp.float32)
    position = jnp.maximum(slot_place, 0)
    row_ids = (position // COLS_DEV).astype(jnp.int32)
    col_ids = (position % COLS_DEV).astype(jnp.int32)
    row_onehot = (row_ids[:, None] == jnp.arange(D // BLK, dtype=jnp.int32)[None, :]).astype(jnp.float32) * live_flag[:, None]
    col_onehot = (col_ids[:, None] == jnp.arange(COLS_DEV, dtype=jnp.int32)[None, :]).astype(jnp.float32) * live_flag[:, None]
    return (row_ids, col_ids, row_onehot, col_onehot, live_flag)

def to_columns(per_slot, col_onehot):
    return jnp.einsum('tsn,sc->tcn', per_slot, col_onehot, precision=highest)

def to_rows(per_slot, row_onehot):
    summed = jnp.einsum('tsk,sr->trk', per_slot, row_onehot, precision=highest)
    return summed.reshape(per_slot.shape[0], D)

def product(form, left, right):
    return jnp.einsum(form, left.astype(jnp.float32), right.astype(jnp.float32), precision=highest)

def rounded_terms(values):
    stored = lax.optimization_barrier(values.astype(jnp.bfloat16))
    return stored.astype(jnp.float32)

def section_pass(acts, cotangent, section_gains, gate_w, up_w, down_w, slot_place):
    inputs = acts.astype(jnp.float32)
    scale_in = lax.rsqrt(lax.optimization_barrier(jnp.mean(inputs * inputs, axis=-1, keepdims=True)) + epsilon)
    normed_in = inputs * scale_in
    normed = (normed_in * section_gains[0]).astype(jnp.bfloat16)
    normed_blocks = normed.reshape(TOKENS, D // BLK, BLK)

    def forward_device(branch_sum, device):
        gate_dev, up_dev, down_dev, place = device
        row_ids, col_ids, row_onehot, col_onehot, live_flag = slot_tables(place)
        picked_in = jnp.take(normed_blocks, row_ids, axis=1)
        gate_sum = to_columns(product('tsk,skn->tsn', picked_in, gate_dev), col_onehot)
        up_sum = to_columns(product('tsk,skn->tsn', picked_in, up_dev), col_onehot)
        hidden = (jax.nn.silu(gate_sum) * up_sum).astype(jnp.bfloat16)
        picked_hidden = jnp.take(hidden, col_ids, axis=1)
        slot_terms = rounded_terms(product('tsn,snk->tsk', picked_hidden, down_dev))
        return (branch_sum + to_rows(slot_terms, row_onehot), (gate_sum, up_sum, hidden))
    branch, saved = lax.scan(forward_device, jnp.zeros((TOKENS, D), jnp.float32), (gate_w, up_w, down_w, slot_place))
    scale_out = lax.rsqrt(lax.optimization_barrier(jnp.mean(branch * branch, axis=-1, keepdims=True)) + epsilon)
    unit_branch = branch * scale_out
    layer_out = (inputs + unit_branch * section_gains[1]).astype(jnp.bfloat16)
    grad_out = cotangent.astype(jnp.float32)
    scaled = grad_out * section_gains[1]
    grad_branch = (scale_out * (scaled - unit_branch * lax.optimization_barrier(jnp.mean(scaled * unit_branch, axis=-1, keepdims=True)))).astype(jnp.bfloat16)
    grad_blocks = grad_branch.reshape(TOKENS, D // BLK, BLK)

    def backward_device(normed_sum, device):
        gate_dev, up_dev, down_dev, place, gate_part, up_part, hidden_part = device
        row_ids, col_ids, row_onehot, col_onehot, live_flag = slot_tables(place)
        picked_in = jnp.take(normed_blocks, row_ids, axis=1)
        picked_grad = jnp.take(grad_blocks, row_ids, axis=1)
        picked_hidden = jnp.take(hidden_part, col_ids, axis=1)
        grad_hidden = to_columns(product('tsk,snk->tsn', picked_grad, down_dev), col_onehot)
        down_part = (product('tsn,tsk->snk', picked_hidden, picked_grad) * live_flag[:, None, None]).astype(jnp.bfloat16)
        sigmoid_gate = jax.nn.sigmoid(gate_part)
        grad_gate = (grad_hidden * up_part * sigmoid_gate * (1.0 + gate_part * (1.0 - sigmoid_gate))).astype(jnp.bfloat16)
        grad_up = (grad_hidden * gate_part * sigmoid_gate).astype(jnp.bfloat16)
        picked_gate = jnp.take(grad_gate, col_ids, axis=1)
        picked_up = jnp.take(grad_up, col_ids, axis=1)
        gate_part_grad = (product('tsk,tsn->skn', picked_in, picked_gate) * live_flag[:, None, None]).astype(jnp.bfloat16)
        up_part_grad = (product('tsk,tsn->skn', picked_in, picked_up) * live_flag[:, None, None]).astype(jnp.bfloat16)
        mixed_sum = product('tsn,skn->tsk', picked_gate, gate_dev) + product('tsn,skn->tsk', picked_up, up_dev)
        slot_terms = rounded_terms(mixed_sum)
        return (normed_sum + to_rows(slot_terms, row_onehot), (gate_part_grad, up_part_grad, down_part))
    grad_normed, grads = lax.scan(backward_device, jnp.zeros((TOKENS, D), jnp.float32), (gate_w, up_w, down_w, slot_place) + saved)
    gate_grad, up_grad, down_grad = grads
    scaled_in = grad_normed * section_gains[0]
    input_grad = (grad_out + scale_in * (scaled_in - normed_in * lax.optimization_barrier(jnp.mean(scaled_in * normed_in, axis=-1, keepdims=True)))).astype(jnp.bfloat16)
    gain_grad = jnp.stack([lax.optimization_barrier(jnp.sum(grad_normed * normed_in, axis=0)), lax.optimization_barrier(jnp.sum(grad_out * unit_branch, axis=0))])
    return (layer_out, input_grad, gate_grad, up_grad, down_grad, gain_grad)

def reference(acts, cotangent, gains, gate_blocks, up_blocks, down_blocks, block_place):
    layer_list, input_list, gate_list, up_list, down_list, gain_list = ([], [], [], [], [], [])
    for section_id in range(N_SECTION):
        first_row = section_id * TOKENS
        results = section_pass(acts[first_row:first_row + TOKENS], cotangent[first_row:first_row + TOKENS], gains[section_id], gate_blocks[section_id].reshape(N_TP, SLOTS, BLK, BLK), up_blocks[section_id].reshape(N_TP, SLOTS, BLK, BLK), down_blocks[section_id].reshape(N_TP, SLOTS, BLK, BLK), block_place[section_id].reshape(N_TP, SLOTS))
        layer_list.append(results[0])
        input_list.append(results[1])
        gate_list.append(results[2].reshape(N_TP * SLOTS, BLK, BLK))
        up_list.append(results[3].reshape(N_TP * SLOTS, BLK, BLK))
        down_list.append(results[4].reshape(N_TP * SLOTS, BLK, BLK))
        gain_list.append(results[5])
    shifted = input_list[1:] + [jnp.zeros((TOKENS, D), jnp.bfloat16)]
    return (jnp.concatenate(layer_list, axis=0), jnp.concatenate(shifted, axis=0), jnp.stack(gate_list), jnp.stack(up_list), jnp.stack(down_list), jnp.stack(gain_list))
```

```python
import functools

import jax
import jax.numpy as jnp
from jax import lax
from jax.experimental import pallas as pl
from jax.experimental.pallas import tpu as pltpu
from jax.sharding import Mesh
from jax.sharding import PartitionSpec as P

epsilon = 1e-05
f32 = jnp.float32
bf16 = jnp.bfloat16
B = 128


def dot(left, right, contract):
    return lax.dot_general(left, right, ((contract[:1], contract[1:]), ((), ())), preferred_element_type=f32)


def block_cols(index):
    return slice(index * B, (index + 1) * B)


def slot_place(place_ref, half, peer, group, slot, peers, slots):
    return place_ref[0, ((half ^ group) * peers + peer) * slots + slot]


def feature_block(place):
    return lax.shift_right_logical(jnp.maximum(place, 0), 1)


def column_masks(place):
    live = place >= 0
    odd = (place & 1) == 1
    first = jnp.where(live & jnp.logical_not(odd), 1.0, 0.0).astype(f32)
    second = jnp.where(live & odd, 1.0, 0.0).astype(f32)
    return first, second


def scaled_block(block, factor):
    return (block.astype(f32) * factor).astype(bf16)


def pick_blocks(place_ref, blocks_ref, out_ref, half, peers, slots):
    def one_peer(peer, carry):
        for group in range(2):
            for slot in range(slots):
                place = slot_place(place_ref, half, peer, group, slot, peers, slots)
                out_ref[peer, :, block_cols(group * slots + slot)] = blocks_ref[feature_block(place)]
        return carry

    lax.fori_loop(0, peers, one_peer, 0)


def sum_blocks(place_ref, got_ref, total_ref, half, peers, slots):
    total_ref[...] = jnp.zeros_like(total_ref)

    def one_peer(peer, carry):
        for group in range(2):
            for slot in range(slots):
                place = slot_place(place_ref, half, peer, group, slot, peers, slots)
                row = feature_block(place)
                term = got_ref[peer, :, block_cols(group * slots + slot)].astype(f32)
                total_ref[row] = total_ref[row] + term
        return carry

    lax.fori_loop(0, peers, one_peer, 0)


def inverse_norm(squares, width):
    return lax.rsqrt(squares / width + epsilon)


def send_normed(slots, place_ref, acts_ref, gains_ref, out_ref, blocks_ref):
    peers = out_ref.shape[0]
    half = lax.axis_index("half")
    inputs = acts_ref[...].astype(f32)
    scale_in = inverse_norm(jnp.sum(inputs * inputs, axis=1, keepdims=True), inputs.shape[1])
    normed = (inputs * scale_in * gains_ref[0, 0:1, :]).astype(bf16)
    for row in range(blocks_ref.shape[0]):
        blocks_ref[row] = normed[:, block_cols(row)]
    pick_blocks(place_ref, blocks_ref, out_ref, half, peers, slots)


def masked_weights(place_ref, half, peer, group, peers, gate_ref, up_ref, down_ref):
    slots = gate_ref.shape[1]
    ins, downs = [], []
    for slot in range(slots):
        place = slot_place(place_ref, half, peer, group, slot, peers, slots)
        first, second = column_masks(place)
        gate, up, down = gate_ref[0, slot], up_ref[0, slot], down_ref[0, slot]
        ins.append(
            jnp.concatenate(
                [
                    scaled_block(gate, first),
                    scaled_block(gate, second),
                    scaled_block(up, first),
                    scaled_block(up, second),
                ],
                axis=1,
            )
        )
        downs.append(jnp.concatenate([scaled_block(down, first), scaled_block(down, second)], axis=0))
    return jnp.concatenate(ins, axis=0), jnp.concatenate(downs, axis=1)


def forward(
    place_ref, got_ref, gate0, up0, down0, gate1, up1, down1, terms_ref, hidden_ref, dgate_ref, dup_ref
):
    peers, rows, _ = got_ref.shape
    slots = gate0.shape[1]
    wide = slots * B
    half, peer = lax.axis_index("half"), lax.axis_index("peer")
    for group, (gate, up, down) in enumerate(((gate0, up0, down0), (gate1, up1, down1))):
        w_in, w_down = masked_weights(place_ref, half, peer, group, peers, gate, up, down)
        picked = got_ref[:, :, group * wide : (group + 1) * wide].reshape(peers * rows, wide)
        sums = dot(picked, w_in, (1, 0))
        gate_sum, up_sum = sums[:, : 2 * B], sums[:, 2 * B :]
        sigmoid = jax.nn.sigmoid(gate_sum)
        silu = gate_sum * sigmoid
        hidden = (silu * up_sum).astype(bf16)
        terms = dot(hidden, w_down, (1, 0)).astype(bf16)
        terms_ref[:, :, group * wide : (group + 1) * wide] = terms.reshape(peers, rows, wide)
        hidden_ref[group] = hidden
        dgate_ref[group] = up_sum * sigmoid * (1.0 + gate_sum * (1.0 - sigmoid))
        dup_ref[group] = silu


def middle(
    slots, place_ref, got_ref, acts_ref, cot_ref, gains_ref, layer_ref, out_ref, total_ref, blocks_ref
):
    peers = got_ref.shape[0]
    rows, width = acts_ref.shape
    half = lax.axis_index("half")
    sum_blocks(place_ref, got_ref, total_ref, half, peers, slots)
    branch = total_ref[...]
    squares = jnp.sum(jnp.sum(branch * branch, axis=0), axis=1, keepdims=True)
    scale_out = inverse_norm(squares, width)
    row_id = lax.broadcasted_iota(jnp.int32, (rows, B), 0)
    mixed = jnp.zeros((rows, B), f32)
    for block in range(width // B):
        cols = block_cols(block)
        grad = cot_ref[:, cols].astype(f32)
        unit = total_ref[block] * scale_out
        gain = gains_ref[0, 1:2, cols]
        layer_ref[:, cols] = (acts_ref[:, cols].astype(f32) + unit * gain).astype(bf16)
        mixed = mixed + grad * gain * unit
        part = jnp.sum(grad * unit, axis=0, keepdims=True)
        high = part.astype(bf16).astype(f32)
        aside = jnp.where(row_id == 0, high, jnp.where(row_id == 1, part - high, 0.0))
        out_ref[block, :, 2 * slots * B :] = aside.astype(bf16)
    mean = jnp.sum(mixed, axis=1, keepdims=True) / width
    for block in range(width // B):
        cols = block_cols(block)
        scaled = cot_ref[:, cols].astype(f32) * gains_ref[0, 1:2, cols]
        unit = total_ref[block] * scale_out
        blocks_ref[block] = (scale_out * (scaled - unit * mean)).astype(bf16)
    pick_blocks(place_ref, blocks_ref, out_ref, half, peers, slots)


def backward(
    place_ref, got_ref, picked_ref, gate0, up0, down0, gate1, up1, down1, dgate_ref, dup_ref, out_ref, grads_ref
):
    peers, rows, _ = got_ref.shape
    slots = gate0.shape[1]
    wide = slots * B
    half, peer = lax.axis_index("half"), lax.axis_index("peer")
    parts = []
    for group, (gate, up, down) in enumerate(((gate0, up0, down0), (gate1, up1, down1))):
        w_in, w_down = masked_weights(place_ref, half, peer, group, peers, gate, up, down)
        cols = slice(group * wide, (group + 1) * wide)
        grad = got_ref[:, :, cols].reshape(peers * rows, wide)
        grad_hidden = dot(grad, w_down, (1, 1))
        both = jnp.concatenate([grad_hidden * dgate_ref[group], grad_hidden * dup_ref[group]], axis=1).astype(bf16)
        grads_ref[group] = both
        back = dot(both, w_in, (1, 1))
        out_ref[:, :, cols] = back.astype(bf16).reshape(peers, rows, wide)
        normed = picked_ref[:, :, cols].reshape(peers * rows, wide).astype(f32)
        part = jnp.sum(normed * back, axis=0, keepdims=True)
        parts.extend(part[:, block_cols(slot)] for slot in range(slots))
    aside = jnp.sum(got_ref[:, :, 2 * wide :].astype(f32), axis=0)
    parts.append(aside[0:1] + aside[1:2])
    row_id = lax.broadcasted_iota(jnp.int32, (rows, B), 0)
    sent = jnp.zeros((rows, B), f32)
    for index, part in enumerate(parts):
        high = part.astype(bf16).astype(f32)
        sent = jnp.where(row_id == 2 * index, high, sent)
        sent = jnp.where(row_id == 2 * index + 1, part - high, sent)
    out_ref[:, :, 2 * wide :] = jnp.broadcast_to(sent.astype(bf16)[None], (peers, rows, B))


def weight_grads(place_ref, got_ref, picked_ref, hidden_ref, grads_ref, own_ref, other_ref):
    peers, rows, _ = got_ref.shape
    slots = own_ref.shape[1]
    wide = slots * B
    half, peer = lax.axis_index("half"), lax.axis_index("peer")
    for group in (1, 0):
        target = (own_ref, other_ref)[group]
        cols = slice(group * wide, (group + 1) * wide)
        grad = got_ref[:, :, cols].reshape(peers * rows, wide)
        picked = picked_ref[:, :, cols].reshape(peers * rows, wide)
        down = dot(hidden_ref[group], grad, (0, 0))
        ins = dot(picked, grads_ref[group], (0, 0))
        for slot in range(slots):
            place = slot_place(place_ref, half, peer, group, slot, peers, slots)
            first, second = column_masks(place)
            line = ins[block_cols(slot)]
            gate = line[:, block_cols(0)] * first + line[:, block_cols(1)] * second
            up = line[:, block_cols(2)] * first + line[:, block_cols(3)] * second
            lane = down[:, block_cols(slot)]
            into = lane[block_cols(0)] * first + lane[block_cols(1)] * second
            for kind, value in enumerate((gate, up, into)):
                target[kind, slot] = value.astype(target.dtype)


def last(
    slots, place_ref, got_ref, acts_ref, cot_ref, gains_ref, grad_ref, gain_ref, total_ref, gain_total_ref
):
    peers = got_ref.shape[0]
    rows, width = acts_ref.shape
    half = lax.axis_index("half")
    sum_blocks(place_ref, got_ref, total_ref, half, peers, slots)
    gain_total_ref[...] = jnp.zeros_like(gain_total_ref)
    for peer in range(peers):
        aside = got_ref[peer, :, 2 * slots * B :].astype(f32)
        for group in range(2):
            for slot in range(slots):
                place = slot_place(place_ref, half, peer, group, slot, peers, slots)
                row = feature_block(place)
                at = 2 * (group * slots + slot)
                gain_total_ref[row] = gain_total_ref[row] + (aside[at : at + 1] + aside[at + 1 : at + 2])
        at = 4 * slots
        gain_ref[1:2, block_cols(peer)] = aside[at : at + 1] + aside[at + 1 : at + 2]
    inputs = acts_ref[...].astype(f32)
    scale_in = inverse_norm(jnp.sum(inputs * inputs, axis=1, keepdims=True), width)
    mixed = jnp.zeros((rows, B), f32)
    for block in range(width // B):
        cols = block_cols(block)
        normed_in = acts_ref[:, cols].astype(f32) * scale_in
        gain = gains_ref[0, 0:1, cols]
        mixed = mixed + total_ref[block] * gain * normed_in
        gain_ref[0:1, cols] = gain_total_ref[block] / gain
    mean = jnp.sum(mixed, axis=1, keepdims=True) / width
    for block in range(width // B):
        cols = block_cols(block)
        normed_in = acts_ref[:, cols].astype(f32) * scale_in
        scaled_in = total_ref[block] * gains_ref[0, 0:1, cols]
        grad = cot_ref[:, cols].astype(f32)
        grad_ref[:, cols] = (grad + scale_in * (scaled_in - normed_in * mean)).astype(bf16)


def finish(own_ref, other_ref, gain_ref, gain_other_ref, gate_ref, up_ref, down_ref, gain_out_ref):
    for kind, target in enumerate((gate_ref, up_ref, down_ref)):
        target[0] = (own_ref[kind] + other_ref[kind].astype(f32)).astype(bf16)
    gain_out_ref[0] = gain_ref[...] + gain_other_ref[...]


def call(kernel, name, outs, operands, scratch=()):
    vmem = pl.BlockSpec(memory_space=pltpu.VMEM)
    specs = [pl.BlockSpec(memory_space=pltpu.SMEM) if o.dtype == jnp.int32 else vmem for o in operands]
    shapes = [jax.ShapeDtypeStruct(shape, dtype) for shape, dtype in outs]
    return pl.pallas_call(
        kernel,
        name=name,
        out_shape=shapes,
        in_specs=specs,
        out_specs=[vmem] * len(shapes),
        scratch_shapes=list(scratch),
        compiler_params=pltpu.CompilerParams(vmem_limit_bytes=40 * 1024 * 1024),
    )(*operands)


def body(acts, cotangent, gains, gate_blocks, up_blocks, down_blocks, block_place):
    rows, width = acts.shape
    slots = gate_blocks.shape[1]
    peers = lax.axis_size("peer")
    features = width // B
    pairs = 2 * slots * B
    tokens = peers * rows

    def to_other(value):
        return lax.ppermute(value, "half", [(0, 1), (1, 0)])

    def exchange(value):
        return lax.all_to_all(value, "peer", split_axis=0, concat_axis=0, tiled=True)

    own = (gate_blocks, up_blocks, down_blocks)
    other = tuple(to_other(value) for value in own)
    feature_sums = pltpu.VMEM((features, rows, B), f32)
    feature_blocks = pltpu.VMEM((features, rows, B), bf16)

    (sent,) = call(
        functools.partial(send_normed, slots),
        "send_normed",
        [((peers, rows, pairs), bf16)],
        (block_place, acts, gains),
        [feature_blocks],
    )
    picked = exchange(sent)
    terms, hidden, dgate, dup = call(
        forward,
        "forward",
        [
            ((peers, rows, pairs), bf16),
            ((2, tokens, 2 * B), bf16),
            ((2, tokens, 2 * B), f32),
            ((2, tokens, 2 * B), f32),
        ],
        (block_place, picked, *own, *other),
    )
    layer_out, grad_sent = call(
        functools.partial(middle, slots),
        "middle",
        [((rows, width), bf16), ((peers, rows, pairs + B), bf16)],
        (block_place, exchange(terms), acts, cotangent, gains),
        [feature_sums, feature_blocks],
    )
    grad_got = exchange(grad_sent)
    back_sent, grads = call(
        backward,
        "backward",
        [((peers, rows, pairs + B), bf16), ((2, tokens, 4 * B), bf16)],
        (block_place, grad_got, picked, *own, *other, dgate, dup),
    )
    back_got = exchange(back_sent)
    own_grads, other_grads = call(
        weight_grads,
        "weight_grads",
        [((3, slots, B, B), f32), ((3, slots, B, B), bf16)],
        (block_place, grad_got, picked, hidden, grads),
    )
    grads_got = to_other(other_grads)
    input_grad, gain_half = call(
        functools.partial(last, slots),
        "last",
        [((rows, width), bf16), ((2, width), f32)],
        (block_place, back_got, acts, cotangent, gains),
        [feature_sums, pltpu.VMEM((features, 1, B), f32)],
    )
    count = lax.axis_size("section")
    grad_back = lax.ppermute(input_grad, "section", [(source, source - 1) for source in range(1, count)])
    gain_other = to_other(gain_half)
    gate_grad, up_grad, down_grad, gain_grad = call(
        finish,
        "finish",
        [((1, slots, B, B), bf16)] * 3 + [((1, 2, width), f32)],
        (own_grads, grads_got, gain_half, gain_other),
    )
    return (layer_out, grad_back, gate_grad, up_grad, down_grad, gain_grad)


def solution(mesh):
    sections, devices = mesh.devices.shape
    split = Mesh(mesh.devices.reshape(sections, 2, devices // 2), ("section", "half", "peer"))
    tp = ("half", "peer")
    tokens = P(("section", *tp), None)
    blocks = P("section", tp, None, None)
    return jax.shard_map(
        body,
        mesh=split,
        in_specs=(tokens, tokens, P("section", None, None), blocks, blocks, blocks, P("section", None)),
        out_specs=(tokens, tokens, blocks, blocks, blocks, P("section", None, None)),
        check_vma=False,
    )
```

```python
import functools

import jax
import jax.numpy as jnp
from jax import lax
from jax.experimental import pallas as pl
from jax.experimental.pallas import tpu as pltpu
from jax.sharding import Mesh
from jax.sharding import PartitionSpec as P

epsilon = 1e-05
f32 = jnp.float32
bf16 = jnp.bfloat16
B = 128
SUMS = 3
ASIDE = 8


def dot(left, right, contract):
    return lax.dot_general(left, right, ((contract[:1], contract[1:]), ((), ())), preferred_element_type=f32)


def block_cols(index):
    return slice(index * B, (index + 1) * B)


def slot_place(place_ref, half, peer, group, slot, peers, slots):
    return place_ref[0, ((half ^ group) * peers + peer) * slots + slot]


def feature_block(place):
    return lax.shift_right_logical(jnp.maximum(place, 0), 1)


def column_masks(place):
    live = place >= 0
    odd = (place & 1) == 1
    first = jnp.where(live & jnp.logical_not(odd), 1.0, 0.0).astype(f32)
    second = jnp.where(live & odd, 1.0, 0.0).astype(f32)
    return first, second


def scaled_block(block, factor):
    return (block.astype(f32) * factor).astype(bf16)


def pick_blocks(place_ref, blocks_ref, out_ref, half, peers, slots):
    for peer in range(peers):
        for group in range(2):
            for slot in range(slots):
                place = slot_place(place_ref, half, peer, group, slot, peers, slots)
                out_ref[peer, :, block_cols(group * slots + slot)] = blocks_ref[feature_block(place)]


def sum_blocks(place_ref, got_ref, total_refs, half, peers, slots):
    for total_ref in total_refs:
        total_ref[...] = jnp.zeros_like(total_ref)
    count = 0
    for peer in range(peers):
        for group in range(2):
            for slot in range(slots):
                place = slot_place(place_ref, half, peer, group, slot, peers, slots)
                row = feature_block(place)
                total_ref = total_refs[count % len(total_refs)]
                count += 1
                term = got_ref[peer, :, block_cols(group * slots + slot)].astype(f32)
                total_ref[row] = total_ref[row] + term
    for total_ref in total_refs[1:]:
        total_refs[0][...] += total_ref[...]


def inverse_norm(squares, width):
    return lax.rsqrt(squares / width + epsilon)


def send_normed(
    slots, place_ref, acts_ref, gains_ref, out_ref, blocks_ref
):
    peers = out_ref.shape[0]
    half = lax.axis_index("za")
    inputs = acts_ref[...].astype(f32)
    scale_in = inverse_norm(jnp.sum(inputs * inputs, axis=1, keepdims=True), inputs.shape[1])
    normed = (inputs * scale_in * gains_ref[0, 0:1, :]).astype(bf16)
    for row in range(blocks_ref.shape[0]):
        blocks_ref[row] = normed[:, block_cols(row)]
    pick_blocks(place_ref, blocks_ref, out_ref, half, peers, slots)


def own_peer():
    return lax.axis_index("zb") * lax.axis_size("xc") + lax.axis_index("xc")


def masked_weights(place_ref, half, peer, group, peers, weights):
    gate_ref, up_ref, down_ref = weights[3 * group : 3 * group + 3]
    slots = gate_ref.shape[1]
    ins, downs = [], []
    for slot in range(slots):
        place = slot_place(place_ref, half, peer, group, slot, peers, slots)
        first, second = column_masks(place)
        gate, up, down = gate_ref[0, slot], up_ref[0, slot], down_ref[0, slot]
        ins.append(
            jnp.concatenate(
                [
                    scaled_block(gate, first),
                    scaled_block(gate, second),
                    scaled_block(up, first),
                    scaled_block(up, second),
                ],
                axis=1,
            )
        )
        downs.append(jnp.concatenate([scaled_block(down, first), scaled_block(down, second)], axis=0))
    return jnp.concatenate(ins, axis=0), jnp.concatenate(downs, axis=1)


def forward(
    place_ref, got_ref, gate0, up0, down0, gate1, up1, down1, terms_ref, hidden_ref, dgate_ref, dup_ref
):
    peers, rows, _ = got_ref.shape
    weights = (gate0, up0, down0, gate1, up1, down1)
    slots = gate0.shape[1]
    wide = slots * B
    half, peer = lax.axis_index("za"), own_peer()
    for group in range(2):
        w_in, w_down = masked_weights(place_ref, half, peer, group, peers, weights)
        picked = got_ref[:, :, group * wide : (group + 1) * wide].reshape(peers * rows, wide)
        sums = dot(picked, w_in, (1, 0))
        gate_sum, up_sum = sums[:, : 2 * B], sums[:, 2 * B :]
        sigmoid = jax.nn.sigmoid(gate_sum)
        silu = gate_sum * sigmoid
        hidden = (silu * up_sum).astype(bf16)
        terms = dot(hidden, w_down, (1, 0)).astype(bf16)
        terms_ref[:, :, group * wide : (group + 1) * wide] = terms.reshape(peers, rows, wide)
        hidden_ref[group] = hidden
        dgate_ref[group] = up_sum * sigmoid * (1.0 + gate_sum * (1.0 - sigmoid))
        dup_ref[group] = silu


def middle(
    slots,
    place_ref,
    got_ref,
    acts_ref,
    cot_ref,
    gains_ref,
    layer_ref,
    out_ref,
    blocks_ref,
    total_ref,
    *more_refs,
):
    peers = got_ref.shape[0]
    rows, width = acts_ref.shape
    half = lax.axis_index("za")
    sum_blocks(place_ref, got_ref, (total_ref, *more_refs), half, peers, slots)
    branch = total_ref[...]
    squares = jnp.sum(jnp.sum(branch * branch, axis=0), axis=1, keepdims=True)
    scale_out = inverse_norm(squares, width)
    row_id = lax.broadcasted_iota(jnp.int32, (rows, B), 0)
    mixed = jnp.zeros((rows, B), f32)
    for block in range(width // B):
        cols = block_cols(block)
        grad = cot_ref[:, cols].astype(f32)
        unit = total_ref[block] * scale_out
        gain = gains_ref[0, 1:2, cols]
        layer_ref[:, cols] = (acts_ref[:, cols].astype(f32) + unit * gain).astype(bf16)
        mixed = mixed + grad * gain * unit
        part = jnp.sum(grad * unit, axis=0, keepdims=True)
        high = part.astype(bf16).astype(f32)
        aside = jnp.where(row_id == 0, high, jnp.where(row_id == 1, part - high, 0.0))
        out_ref[block, :, 2 * slots * B :] = aside.astype(bf16)
    mean = jnp.sum(mixed, axis=1, keepdims=True) / width
    for block in range(width // B):
        cols = block_cols(block)
        scaled = cot_ref[:, cols].astype(f32) * gains_ref[0, 1:2, cols]
        unit = total_ref[block] * scale_out
        blocks_ref[block] = (scale_out * (scaled - unit * mean)).astype(bf16)
    pick_blocks(place_ref, blocks_ref, out_ref, half, peers, slots)


def backward(
    place_ref,
    got_ref,
    picked_ref,
    gate0,
    up0,
    down0,
    gate1,
    up1,
    down1,
    hidden_ref,
    dgate_ref,
    dup_ref,
    out_ref,
    own_grad_ref,
    other_grad_ref,
):
    peers, rows, _ = got_ref.shape
    weights = (gate0, up0, down0, gate1, up1, down1)
    slots = gate0.shape[1]
    wide = slots * B
    half, peer = lax.axis_index("za"), own_peer()
    parts = []
    for group in range(2):
        w_in, w_down = masked_weights(place_ref, half, peer, group, peers, weights)
        cols = slice(group * wide, (group + 1) * wide)
        grad = got_ref[:, :, cols].reshape(peers * rows, wide)
        grad_hidden = dot(grad, w_down, (1, 1))
        both = jnp.concatenate([grad_hidden * dgate_ref[group], grad_hidden * dup_ref[group]], axis=1).astype(bf16)
        back = dot(both, w_in, (1, 1))
        out_ref[:, :, cols] = back.astype(bf16).reshape(peers, rows, wide)
        picked = picked_ref[:, :, cols].reshape(peers * rows, wide)
        ins = dot(picked, both, (0, 0))
        down = dot(hidden_ref[group], grad, (0, 0))
        target = (own_grad_ref, other_grad_ref)[group]
        for slot in range(slots):
            place = slot_place(place_ref, half, peer, group, slot, peers, slots)
            first, second = column_masks(place)
            line = ins[block_cols(slot)]
            lane = down[:, block_cols(slot)]
            target[0, slot] = (line[:, block_cols(0)] * first + line[:, block_cols(1)] * second).astype(target.dtype)
            target[1, slot] = (line[:, block_cols(2)] * first + line[:, block_cols(3)] * second).astype(target.dtype)
            target[2, slot] = (lane[block_cols(0)] * first + lane[block_cols(1)] * second).astype(target.dtype)
        part = jnp.sum(picked.astype(f32) * back, axis=0, keepdims=True)
        parts.extend(part[:, block_cols(slot)] for slot in range(slots))
    aside = jnp.sum(got_ref[:, :, 2 * wide :].astype(f32), axis=0)
    parts.append(aside[0:1] + aside[1:2])
    row_id = lax.broadcasted_iota(jnp.int32, (rows, B), 0)
    sent = jnp.zeros((rows, B), f32)
    for index, part in enumerate(parts):
        high = part.astype(bf16).astype(f32)
        sent = jnp.where(row_id == index, high, sent)
        sent = jnp.where(row_id == ASIDE + index, part - high, sent)
    out_ref[:, :, 2 * wide :] = jnp.broadcast_to(sent.astype(bf16)[None], (peers, rows, B))


def last(
    slots,
    place_ref,
    got_ref,
    acts_ref,
    cot_ref,
    gains_ref,
    grad_ref,
    gain_ref,
    total_ref,
    *more_refs,
):
    peers = got_ref.shape[0]
    rows, width = acts_ref.shape
    half = lax.axis_index("za")
    gain_refs = more_refs[-SUMS:]
    sum_blocks(place_ref, got_ref, (total_ref, *more_refs[:-SUMS]), half, peers, slots)
    for gain_total_ref in gain_refs:
        gain_total_ref[...] = jnp.zeros_like(gain_total_ref)
    for peer in range(peers):
        aside = got_ref[peer, :, 2 * slots * B :].astype(f32)
        aside = aside[:ASIDE] + aside[ASIDE:]
        for group in range(2):
            for slot in range(slots):
                place = slot_place(place_ref, half, peer, group, slot, peers, slots)
                row = feature_block(place)
                at = group * slots + slot
                gain_total_ref = gain_refs[at % SUMS]
                gain_total_ref[row] = gain_total_ref[row] + aside[at : at + 1]
        gain_ref[1:2, block_cols(peer)] = aside[2 * slots : 2 * slots + 1]
    inputs = acts_ref[...].astype(f32)
    scale_in = inverse_norm(jnp.sum(inputs * inputs, axis=1, keepdims=True), width)
    mixed = jnp.zeros((rows, B), f32)
    for block in range(width // B):
        cols = block_cols(block)
        normed_in = acts_ref[:, cols].astype(f32) * scale_in
        gain = gains_ref[0, 0:1, cols]
        mixed = mixed + total_ref[block] * gain * normed_in
        gain_ref[0:1, cols] = sum(ref[block] for ref in gain_refs) / gain
    mean = jnp.sum(mixed, axis=1, keepdims=True) / width
    for block in range(width // B):
        cols = block_cols(block)
        normed_in = acts_ref[:, cols].astype(f32) * scale_in
        scaled_in = total_ref[block] * gains_ref[0, 0:1, cols]
        grad = cot_ref[:, cols].astype(f32)
        grad_ref[:, cols] = (grad + scale_in * (scaled_in - normed_in * mean)).astype(bf16)


def finish(own_ref, other_ref, gain_ref, gain_other_ref, gate_ref, up_ref, down_ref, gain_out):
    for kind, target in enumerate((gate_ref, up_ref, down_ref)):
        target[0] = (own_ref[kind] + other_ref[kind].astype(f32)).astype(bf16)
    gain_out[0] = gain_ref[...] + gain_other_ref[...]


def call(kernel, name, outs, operands, scratch=(), far_in=(), far_out=()):
    near, far = pl.BlockSpec(memory_space=pltpu.VMEM), pl.BlockSpec(memory_space=pl.ANY)
    scalars = pl.BlockSpec(memory_space=pltpu.SMEM)
    specs = [
        far if index in far_in else scalars if value.dtype == jnp.int32 else near
        for index, value in enumerate(operands)
    ]
    return pl.pallas_call(
        kernel,
        name=name,
        out_shape=[jax.ShapeDtypeStruct(shape, dtype) for shape, dtype in outs],
        in_specs=specs,
        out_specs=[far if index in far_out else near for index in range(len(outs))],
        scratch_shapes=list(scratch),
        compiler_params=pltpu.CompilerParams(vmem_limit_bytes=40 * 1024 * 1024),
    )(*operands)


def body(acts, cotangent, gains, gate_blocks, up_blocks, down_blocks, block_place):
    rows, width = acts.shape
    slots = gate_blocks.shape[1]
    peer_axes = ("zb", "xc")
    peers = lax.axis_size(peer_axes)
    features = width // B
    pairs = 2 * slots * B
    tokens = peers * rows

    def to_other(value):
        return lax.ppermute(value, "za", [(0, 1), (1, 0)])

    def exchange(value):
        return lax.all_to_all(value, peer_axes, split_axis=0, concat_axis=0, tiled=True)

    feature_sums = pltpu.VMEM((features, rows, B), f32)
    feature_blocks = pltpu.VMEM((features, rows, B), bf16)

    own = (gate_blocks, up_blocks, down_blocks)
    both = (*own, *(to_other(value) for value in own))
    (sent,) = call(
        functools.partial(send_normed, slots),
        "send_normed",
        [((peers, rows, pairs), bf16)],
        (block_place, acts, gains),
        [feature_blocks],
    )
    picked = exchange(sent)
    terms, hidden, dgate, dup = call(
        forward,
        "forward",
        [
            ((peers, rows, pairs), bf16),
            ((2, tokens, 2 * B), bf16),
            ((2, tokens, 2 * B), f32),
            ((2, tokens, 2 * B), f32),
        ],
        (block_place, picked, *both),
    )
    layer_out, grad_sent = call(
        functools.partial(middle, slots),
        "middle",
        [((rows, width), bf16), ((peers, rows, pairs + B), bf16)],
        (block_place, exchange(terms), acts, cotangent, gains),
        [feature_blocks] + [feature_sums] * SUMS,
    )
    weights = (3, slots, B, B)
    back_sent, own_grads, other_grads = call(
        backward,
        "backward",
        [((peers, rows, pairs + B), bf16), (weights, f32), (weights, bf16)],
        (block_place, exchange(grad_sent), picked, *both, hidden, dgate, dup),
    )
    grads_got = to_other(other_grads)
    input_grad, gain_half = call(
        functools.partial(last, slots),
        "last",
        [((rows, width), bf16), ((2, width), f32)],
        (block_place, exchange(back_sent), acts, cotangent, gains),
        [feature_sums] * SUMS + [pltpu.VMEM((features, 1, B), f32)] * SUMS,
    )
    section = ("y", "zh")
    count = lax.axis_size(section)
    grad_back = lax.ppermute(input_grad, section, [(source, source - 1) for source in range(1, count)])
    gain_other = to_other(gain_half)
    gate_grad, up_grad, down_grad, gain_grad = call(
        finish,
        "finish",
        [((1, slots, B, B), bf16)] * 3 + [((1, 2, width), f32)],
        (own_grads, grads_got, gain_half, gain_other),
    )
    return (layer_out, grad_back, gate_grad, up_grad, down_grad, gain_grad)


def solution(mesh):
    names = ("y", "zh", "za", "zb", "xc")
    split = Mesh(mesh.devices.reshape(4, 2, 2, 4, 8), names)
    section, tp = names[:2], names[2:]
    tokens = P(names, None)
    blocks = P(section, tp, None, None)
    whole = P(section, None, None)
    return jax.shard_map(
        body,
        mesh=split,
        in_specs=(tokens, tokens, whole, blocks, blocks, blocks, P(section, None)),
        out_specs=(tokens, tokens, blocks, blocks, blocks, whole),
        check_vma=False,
    )
```

```python
import functools

import jax
import jax.numpy as jnp
from jax import lax
from jax.experimental import pallas as pl
from jax.experimental.pallas import tpu as pltpu
from jax.sharding import Mesh
from jax.sharding import PartitionSpec as P

epsilon = 1e-05
f32 = jnp.float32
bf16 = jnp.bfloat16
B = 128
SUMS = 3
ASIDE = 8


def dot(left, right, contract):
    return lax.dot_general(left, right, ((contract[:1], contract[1:]), ((), ())), preferred_element_type=f32)


def block_cols(index):
    return slice(index * B, (index + 1) * B)


def slot_rows(index, rows):
    return slice(index * rows, (index + 1) * rows)


def slots_side_by_side(got_ref, group, slots, rows):
    parts = [got_ref[:, slot_rows(group * slots + slot, rows), :] for slot in range(slots)]
    return jnp.concatenate([part.reshape(-1, B) for part in parts], axis=1)


def store_slots(out_ref, values, group, slots, rows):
    for slot in range(slots):
        out_ref[:, slot_rows(group * slots + slot, rows), :] = values[:, block_cols(slot)].reshape(-1, rows, B)


def slot_place(place_ref, half, peer, group, slot, peers, slots):
    return place_ref[0, ((half ^ group) * peers + peer) * slots + slot]


def feature_block(place):
    return lax.shift_right_logical(jnp.maximum(place, 0), 1)


def column_masks(place):
    live = place >= 0
    odd = (place & 1) == 1
    first = jnp.where(live & jnp.logical_not(odd), 1.0, 0.0).astype(f32)
    second = jnp.where(live & odd, 1.0, 0.0).astype(f32)
    return first, second


def scaled_block(block, factor):
    return (block.astype(f32) * factor).astype(bf16)


def pick_blocks(place_ref, blocks_ref, out_ref, half, peers, slots):
    rows = blocks_ref.shape[1]
    for peer in range(peers):
        for group in range(2):
            for slot in range(slots):
                place = slot_place(place_ref, half, peer, group, slot, peers, slots)
                out_ref[peer, slot_rows(group * slots + slot, rows), :] = blocks_ref[feature_block(place)]


def sum_blocks(place_ref, got_ref, total_refs, half, peers, slots):
    for total_ref in total_refs:
        total_ref[...] = jnp.zeros_like(total_ref)
    rows = total_refs[0].shape[1]
    count = 0
    for peer in range(peers):
        for group in range(2):
            for slot in range(slots):
                place = slot_place(place_ref, half, peer, group, slot, peers, slots)
                row = feature_block(place)
                total_ref = total_refs[count % len(total_refs)]
                count += 1
                term = got_ref[peer, slot_rows(group * slots + slot, rows), :].astype(f32)
                total_ref[row] = total_ref[row] + term
    for total_ref in total_refs[1:]:
        total_refs[0][...] += total_ref[...]


def inverse_norm(squares, width):
    return lax.rsqrt(squares / width + epsilon)


def send_normed(
    slots, place_ref, acts_ref, gains_ref, out_ref, blocks_ref
):
    peers = out_ref.shape[0]
    half = lax.axis_index("za")
    inputs = acts_ref[...].astype(f32)
    scale_in = inverse_norm(jnp.sum(inputs * inputs, axis=1, keepdims=True), inputs.shape[1])
    normed = (inputs * scale_in * gains_ref[0, 0:1, :]).astype(bf16)
    for row in range(blocks_ref.shape[0]):
        blocks_ref[row] = normed[:, block_cols(row)]
    pick_blocks(place_ref, blocks_ref, out_ref, half, peers, slots)


def own_peer():
    return lax.axis_index("zb") * lax.axis_size("xc") + lax.axis_index("xc")


def masked_weights(place_ref, half, peer, group, peers, weights):
    gate_ref, up_ref, down_ref = weights[3 * group : 3 * group + 3]
    slots = gate_ref.shape[1]
    ins, downs = [], []
    for slot in range(slots):
        place = slot_place(place_ref, half, peer, group, slot, peers, slots)
        first, second = column_masks(place)
        gate, up, down = gate_ref[0, slot], up_ref[0, slot], down_ref[0, slot]
        ins.append(
            jnp.concatenate(
                [
                    scaled_block(gate, first),
                    scaled_block(gate, second),
                    scaled_block(up, first),
                    scaled_block(up, second),
                ],
                axis=1,
            )
        )
        downs.append(jnp.concatenate([scaled_block(down, first), scaled_block(down, second)], axis=0))
    return jnp.concatenate(ins, axis=0), jnp.concatenate(downs, axis=1)


def forward(
    place_ref, got_ref, gate0, up0, down0, gate1, up1, down1, terms_ref, hidden_ref, dgate_ref, dup_ref
):
    peers = got_ref.shape[0]
    weights = (gate0, up0, down0, gate1, up1, down1)
    slots = gate0.shape[1]
    rows = terms_ref.shape[1] // (2 * slots)
    half, peer = lax.axis_index("za"), own_peer()
    for group in range(2):
        w_in, w_down = masked_weights(place_ref, half, peer, group, peers, weights)
        picked = slots_side_by_side(got_ref, group, slots, rows)
        sums = dot(picked, w_in, (1, 0))
        gate_sum, up_sum = sums[:, : 2 * B], sums[:, 2 * B :]
        sigmoid = jax.nn.sigmoid(gate_sum)
        silu = gate_sum * sigmoid
        hidden = (silu * up_sum).astype(bf16)
        terms = dot(hidden, w_down, (1, 0)).astype(bf16)
        store_slots(terms_ref, terms, group, slots, rows)
        hidden_ref[group] = hidden
        dgate_ref[group] = up_sum * sigmoid * (1.0 + gate_sum * (1.0 - sigmoid))
        dup_ref[group] = silu


def middle(
    slots,
    place_ref,
    got_ref,
    acts_ref,
    cot_ref,
    gains_ref,
    layer_ref,
    out_ref,
    blocks_ref,
    total_ref,
    *more_refs,
):
    peers = got_ref.shape[0]
    rows, width = acts_ref.shape
    half = lax.axis_index("za")
    sum_blocks(place_ref, got_ref, (total_ref, *more_refs), half, peers, slots)
    branch = total_ref[...]
    squares = jnp.sum(jnp.sum(branch * branch, axis=0), axis=1, keepdims=True)
    scale_out = inverse_norm(squares, width)
    row_id = lax.broadcasted_iota(jnp.int32, (ASIDE, B), 0)
    mixed = jnp.zeros((rows, B), f32)
    for block in range(width // B):
        cols = block_cols(block)
        grad = cot_ref[:, cols].astype(f32)
        unit = total_ref[block] * scale_out
        gain = gains_ref[0, 1:2, cols]
        layer_ref[:, cols] = (acts_ref[:, cols].astype(f32) + unit * gain).astype(bf16)
        mixed = mixed + grad * gain * unit
        part = jnp.sum(grad * unit, axis=0, keepdims=True)
        out_ref[block, 2 * slots * rows :, :] = jnp.where(row_id == 0, part, 0.0).astype(bf16)
    mean = jnp.sum(mixed, axis=1, keepdims=True) / width
    for block in range(width // B):
        cols = block_cols(block)
        scaled = cot_ref[:, cols].astype(f32) * gains_ref[0, 1:2, cols]
        unit = total_ref[block] * scale_out
        blocks_ref[block] = (scale_out * (scaled - unit * mean)).astype(bf16)
    pick_blocks(place_ref, blocks_ref, out_ref, half, peers, slots)


def backward(
    place_ref,
    got_ref,
    picked_ref,
    gate0,
    up0,
    down0,
    gate1,
    up1,
    down1,
    hidden_ref,
    dgate_ref,
    dup_ref,
    out_ref,
    own_grad_ref,
    other_grad_ref,
):
    peers = got_ref.shape[0]
    weights = (gate0, up0, down0, gate1, up1, down1)
    slots = gate0.shape[1]
    rows = picked_ref.shape[1] // (2 * slots)
    half, peer = lax.axis_index("za"), own_peer()
    parts = []
    for group in range(2):
        w_in, w_down = masked_weights(place_ref, half, peer, group, peers, weights)
        grad = slots_side_by_side(got_ref, group, slots, rows)
        grad_hidden = dot(grad, w_down, (1, 1))
        both = jnp.concatenate([grad_hidden * dgate_ref[group], grad_hidden * dup_ref[group]], axis=1).astype(bf16)
        back = dot(both, w_in, (1, 1))
        store_slots(out_ref, back.astype(bf16), group, slots, rows)
        picked = slots_side_by_side(picked_ref, group, slots, rows)
        ins = dot(picked, both, (0, 0))
        down = dot(hidden_ref[group], grad, (0, 0))
        target = (own_grad_ref, other_grad_ref)[group]
        for slot in range(slots):
            place = slot_place(place_ref, half, peer, group, slot, peers, slots)
            first, second = column_masks(place)
            line = ins[block_cols(slot)]
            lane = down[:, block_cols(slot)]
            target[0, slot] = (line[:, block_cols(0)] * first + line[:, block_cols(1)] * second).astype(target.dtype)
            target[1, slot] = (line[:, block_cols(2)] * first + line[:, block_cols(3)] * second).astype(target.dtype)
            target[2, slot] = (lane[block_cols(0)] * first + lane[block_cols(1)] * second).astype(target.dtype)
        part = jnp.sum(picked.astype(f32) * back, axis=0, keepdims=True)
        parts.extend(part[:, block_cols(slot)] for slot in range(slots))
    aside = jnp.sum(got_ref[:, 2 * slots * rows :, :].astype(f32), axis=0)
    parts.append(aside[0:1])
    row_id = lax.broadcasted_iota(jnp.int32, (ASIDE, B), 0)
    sent = jnp.zeros((ASIDE, B), f32)
    for index, part in enumerate(parts):
        sent = jnp.where(row_id == index, part, sent)
    out_ref[:, 2 * slots * rows :, :] = jnp.broadcast_to(sent.astype(bf16)[None], (peers, ASIDE, B))


def last(
    slots,
    place_ref,
    got_ref,
    acts_ref,
    cot_ref,
    gains_ref,
    grad_ref,
    gain_ref,
    total_ref,
    *more_refs,
):
    peers = got_ref.shape[0]
    rows, width = acts_ref.shape
    half = lax.axis_index("za")
    gain_refs = more_refs[-SUMS:]
    sum_blocks(place_ref, got_ref, (total_ref, *more_refs[:-SUMS]), half, peers, slots)
    for gain_total_ref in gain_refs:
        gain_total_ref[...] = jnp.zeros_like(gain_total_ref)
    for peer in range(peers):
        aside = got_ref[peer, 2 * slots * rows :, :].astype(f32)
        for group in range(2):
            for slot in range(slots):
                place = slot_place(place_ref, half, peer, group, slot, peers, slots)
                row = feature_block(place)
                at = group * slots + slot
                gain_total_ref = gain_refs[at % SUMS]
                gain_total_ref[row] = gain_total_ref[row] + aside[at : at + 1]
        gain_ref[1:2, block_cols(peer)] = aside[2 * slots : 2 * slots + 1]
    inputs = acts_ref[...].astype(f32)
    scale_in = inverse_norm(jnp.sum(inputs * inputs, axis=1, keepdims=True), width)
    mixed = jnp.zeros((rows, B), f32)
    for block in range(width // B):
        cols = block_cols(block)
        normed_in = acts_ref[:, cols].astype(f32) * scale_in
        gain = gains_ref[0, 0:1, cols]
        mixed = mixed + total_ref[block] * gain * normed_in
        gain_ref[0:1, cols] = sum(ref[block] for ref in gain_refs) / gain
    mean = jnp.sum(mixed, axis=1, keepdims=True) / width
    for block in range(width // B):
        cols = block_cols(block)
        normed_in = acts_ref[:, cols].astype(f32) * scale_in
        scaled_in = total_ref[block] * gains_ref[0, 0:1, cols]
        grad = cot_ref[:, cols].astype(f32)
        grad_ref[:, cols] = (grad + scale_in * (scaled_in - normed_in * mean)).astype(bf16)


def finish(own_ref, other_ref, gain_ref, gain_other_ref, gate_ref, up_ref, down_ref, gain_out):
    for kind, target in enumerate((gate_ref, up_ref, down_ref)):
        target[0] = (own_ref[kind] + other_ref[kind].astype(f32)).astype(bf16)
    gain_out[0] = gain_ref[...] + gain_other_ref[...]


def call(kernel, name, outs, operands, scratch=(), far_in=(), far_out=()):
    near, far = pl.BlockSpec(memory_space=pltpu.VMEM), pl.BlockSpec(memory_space=pl.ANY)
    scalars = pl.BlockSpec(memory_space=pltpu.SMEM)
    specs = [
        far if index in far_in else scalars if value.dtype == jnp.int32 else near
        for index, value in enumerate(operands)
    ]
    return pl.pallas_call(
        kernel,
        name=name,
        out_shape=[jax.ShapeDtypeStruct(shape, dtype) for shape, dtype in outs],
        in_specs=specs,
        out_specs=[far if index in far_out else near for index in range(len(outs))],
        scratch_shapes=list(scratch),
        compiler_params=pltpu.CompilerParams(vmem_limit_bytes=40 * 1024 * 1024),
    )(*operands)


def body(acts, cotangent, gains, gate_blocks, up_blocks, down_blocks, block_place):
    rows, width = acts.shape
    slots = gate_blocks.shape[1]
    peer_axes = ("zb", "xc")
    peers = lax.axis_size(peer_axes)
    features = width // B
    sent_rows = 2 * slots * rows
    tokens = peers * rows

    def to_other(value):
        return lax.ppermute(value, "za", [(0, 1), (1, 0)])

    def exchange(value):
        return lax.all_to_all(value, peer_axes, split_axis=0, concat_axis=0, tiled=True)

    feature_sums = pltpu.VMEM((features, rows, B), f32)
    feature_blocks = pltpu.VMEM((features, rows, B), bf16)

    own = (gate_blocks, up_blocks, down_blocks)
    both = (*own, *(to_other(value) for value in own))
    (sent,) = call(
        functools.partial(send_normed, slots),
        "send_normed",
        [((peers, sent_rows, B), bf16)],
        (block_place, acts, gains),
        [feature_blocks],
    )
    picked = exchange(sent)
    terms, hidden, dgate, dup = call(
        forward,
        "forward",
        [
            ((peers, sent_rows, B), bf16),
            ((2, tokens, 2 * B), bf16),
            ((2, tokens, 2 * B), f32),
            ((2, tokens, 2 * B), f32),
        ],
        (block_place, picked, *both),
    )
    layer_out, grad_sent = call(
        functools.partial(middle, slots),
        "middle",
        [((rows, width), bf16), ((peers, sent_rows + ASIDE, B), bf16)],
        (block_place, exchange(terms), acts, cotangent, gains),
        [feature_blocks] + [feature_sums] * SUMS,
    )
    weights = (3, slots, B, B)
    back_sent, own_grads, other_grads = call(
        backward,
        "backward",
        [((peers, sent_rows + ASIDE, B), bf16), (weights, f32), (weights, bf16)],
        (block_place, exchange(grad_sent), picked, *both, hidden, dgate, dup),
    )
    grads_got = to_other(other_grads)
    input_grad, gain_half = call(
        functools.partial(last, slots),
        "last",
        [((rows, width), bf16), ((2, width), f32)],
        (block_place, exchange(back_sent), acts, cotangent, gains),
        [feature_sums] * SUMS + [pltpu.VMEM((features, 1, B), f32)] * SUMS,
    )
    section = ("y", "zh")
    count = lax.axis_size(section)
    grad_back = lax.ppermute(input_grad, section, [(source, source - 1) for source in range(1, count)])
    gain_other = to_other(gain_half)
    gate_grad, up_grad, down_grad, gain_grad = call(
        finish,
        "finish",
        [((1, slots, B, B), bf16)] * 3 + [((1, 2, width), f32)],
        (own_grads, grads_got, gain_half, gain_other),
    )
    return (layer_out, grad_back, gate_grad, up_grad, down_grad, gain_grad)


def solution(mesh):
    names = ("y", "zh", "za", "zb", "xc")
    split = Mesh(mesh.devices.reshape(4, 2, 2, 4, 8), names)
    section, tp = names[:2], names[2:]
    tokens = P(names, None)
    blocks = P(section, tp, None, None)
    whole = P(section, None, None)
    return jax.shard_map(
        body,
        mesh=split,
        in_specs=(tokens, tokens, whole, blocks, blocks, blocks, P(section, None)),
        out_specs=(tokens, tokens, blocks, blocks, blocks, whole),
        check_vma=False,
    )
```

```python
import functools

import jax
import jax.numpy as jnp
from jax import lax
from jax.experimental import pallas as pl
from jax.experimental.pallas import tpu as pltpu
from jax.sharding import Mesh
from jax.sharding import PartitionSpec as P

epsilon = 1e-05
f32 = jnp.float32
bf16 = jnp.bfloat16
B = 128
SUMS = 3
ASIDE = 8


def dot(left, right, contract):
    return lax.dot_general(left, right, ((contract[:1], contract[1:]), ((), ())), preferred_element_type=f32)


def block_cols(index):
    return slice(index * B, (index + 1) * B)


def slot_rows(index, rows):
    return slice(index * rows, (index + 1) * rows)


def slots_side_by_side(got_ref, group, slots, rows):
    parts = [got_ref[:, slot_rows(group * slots + slot, rows), :] for slot in range(slots)]
    return jnp.concatenate([part.reshape(-1, B) for part in parts], axis=1)


def store_slots(out_ref, values, group, slots, rows):
    for slot in range(slots):
        out_ref[:, slot_rows(group * slots + slot, rows), :] = values[:, block_cols(slot)].reshape(-1, rows, B)


def slot_place(place_ref, half, peer, group, slot, peers, slots):
    return place_ref[0, ((half ^ group) * peers + peer) * slots + slot]


def feature_block(place):
    return lax.shift_right_logical(jnp.maximum(place, 0), 1)


def column_masks(place):
    live = place >= 0
    odd = (place & 1) == 1
    first = jnp.where(live & jnp.logical_not(odd), 1.0, 0.0).astype(f32)
    second = jnp.where(live & odd, 1.0, 0.0).astype(f32)
    return first, second


def scaled_block(block, factor):
    return block * jnp.full(block.shape, factor, f32).astype(bf16)


def pick_blocks(place_ref, blocks_ref, out_ref, half, peers, slots):
    rows = blocks_ref.shape[1]
    for peer in range(peers):
        for group in range(2):
            for slot in range(slots):
                place = slot_place(place_ref, half, peer, group, slot, peers, slots)
                out_ref[peer, slot_rows(group * slots + slot, rows), :] = blocks_ref[feature_block(place)]


def sum_blocks(place_ref, got_ref, total_refs, half, peers, slots):
    for total_ref in total_refs:
        total_ref[...] = jnp.zeros_like(total_ref)
    rows = total_refs[0].shape[1]
    count = 0
    for peer in range(peers):
        for group in range(2):
            for slot in range(slots):
                place = slot_place(place_ref, half, peer, group, slot, peers, slots)
                row = feature_block(place)
                total_ref = total_refs[count % len(total_refs)]
                count += 1
                term = got_ref[peer, slot_rows(group * slots + slot, rows), :].astype(f32)
                total_ref[row] = total_ref[row] + term
    for total_ref in total_refs[1:]:
        total_refs[0][...] += total_ref[...]


def inverse_norm(squares, width):
    return lax.rsqrt(squares / width + epsilon)


def send_normed(
    slots, place_ref, acts_ref, gains_ref, out_ref, blocks_ref
):
    peers = out_ref.shape[0]
    half = lax.axis_index("za")
    inputs = acts_ref[...].astype(f32)
    scale_in = inverse_norm(jnp.sum(inputs * inputs, axis=1, keepdims=True), inputs.shape[1])
    normed = (inputs * scale_in * gains_ref[0, 0:1, :]).astype(bf16)
    for row in range(blocks_ref.shape[0]):
        blocks_ref[row] = normed[:, block_cols(row)]
    pick_blocks(place_ref, blocks_ref, out_ref, half, peers, slots)


def own_peer():
    return lax.axis_index("zb") * lax.axis_size("xc") + lax.axis_index("xc")


def slot_masks(place_ref, half, peer, group, peers, slots):
    return [
        column_masks(slot_place(place_ref, half, peer, group, slot, peers, slots)) for slot in range(slots)
    ]


def masked_in(masks, gate_ref, up_ref):
    lines = []
    for slot, (first, second) in enumerate(masks):
        gate, up = gate_ref[0, slot], up_ref[0, slot]
        parts = [scaled_block(block, mask) for block in (gate, up) for mask in (first, second)]
        lines.append(jnp.concatenate(parts, axis=1))
    return jnp.concatenate(lines, axis=0)


def masked_down(masks, down_ref):
    parts = []
    for slot, (first, second) in enumerate(masks):
        down = down_ref[0, slot]
        parts.append(jnp.concatenate([scaled_block(down, first), scaled_block(down, second)], axis=0))
    return jnp.concatenate(parts, axis=1)


def gates(place_ref, got_ref, gate0, up0, gate1, up1, hidden_ref, dgate_ref, dup_ref):
    peers = got_ref.shape[0]
    slots = gate0.shape[1]
    rows = got_ref.shape[1] // (2 * slots)
    half, peer = lax.axis_index("za"), own_peer()
    for group, (gate, up) in enumerate(((gate0, up0), (gate1, up1))):
        masks = slot_masks(place_ref, half, peer, group, peers, slots)
        picked = slots_side_by_side(got_ref, group, slots, rows)
        sums = dot(picked, masked_in(masks, gate, up), (1, 0))
        gate_sum, up_sum = sums[:, : 2 * B], sums[:, 2 * B :]
        sigmoid = jax.nn.sigmoid(gate_sum)
        silu = gate_sum * sigmoid
        hidden_ref[group] = (silu * up_sum).astype(bf16)
        dgate_ref[group] = up_sum * sigmoid * (1.0 + gate_sum * (1.0 - sigmoid))
        dup_ref[group] = silu


def down_terms(place_ref, hidden_ref, down0, down1, terms_ref):
    peers = terms_ref.shape[0]
    slots = down0.shape[1]
    rows = terms_ref.shape[1] // (2 * slots)
    half, peer = lax.axis_index("za"), own_peer()
    for group, down in enumerate((down0, down1)):
        masks = slot_masks(place_ref, half, peer, group, peers, slots)
        terms = dot(hidden_ref[group], masked_down(masks, down), (1, 0)).astype(bf16)
        store_slots(terms_ref, terms, group, slots, rows)


def middle(
    slots,
    place_ref,
    got_ref,
    acts_ref,
    cot_ref,
    gains_ref,
    layer_ref,
    out_ref,
    blocks_ref,
    total_ref,
    *more_refs,
):
    peers = got_ref.shape[0]
    rows, width = acts_ref.shape
    half = lax.axis_index("za")
    sum_blocks(place_ref, got_ref, (total_ref, *more_refs), half, peers, slots)
    branch = total_ref[...]
    squares = jnp.sum(jnp.sum(branch * branch, axis=0), axis=1, keepdims=True)
    scale_out = inverse_norm(squares, width)
    row_id = lax.broadcasted_iota(jnp.int32, (ASIDE, B), 0)
    mixed = jnp.zeros((rows, B), f32)
    for block in range(width // B):
        cols = block_cols(block)
        grad = cot_ref[:, cols].astype(f32)
        unit = total_ref[block] * scale_out
        gain = gains_ref[0, 1:2, cols]
        layer_ref[:, cols] = (acts_ref[:, cols].astype(f32) + unit * gain).astype(bf16)
        mixed = mixed + grad * gain * unit
        part = jnp.sum(grad * unit, axis=0, keepdims=True)
        out_ref[block, 2 * slots * rows :, :] = jnp.where(row_id == 0, part, 0.0).astype(bf16)
    mean = jnp.sum(mixed, axis=1, keepdims=True) / width
    for block in range(width // B):
        cols = block_cols(block)
        scaled = cot_ref[:, cols].astype(f32) * gains_ref[0, 1:2, cols]
        unit = total_ref[block] * scale_out
        blocks_ref[block] = (scale_out * (scaled - unit * mean)).astype(bf16)
    pick_blocks(place_ref, blocks_ref, out_ref, half, peers, slots)


def backward(
    place_ref,
    got_ref,
    picked_ref,
    gate0,
    up0,
    down0,
    gate1,
    up1,
    down1,
    hidden_ref,
    dgate_ref,
    dup_ref,
    out_ref,
    own_grad_ref,
    other_grad_ref,
):
    peers = got_ref.shape[0]
    slots = gate0.shape[1]
    rows = picked_ref.shape[1] // (2 * slots)
    half, peer = lax.axis_index("za"), own_peer()
    parts = []
    for group, (gate, up, down_w) in enumerate(((gate0, up0, down0), (gate1, up1, down1))):
        masks = slot_masks(place_ref, half, peer, group, peers, slots)
        w_in, w_down = masked_in(masks, gate, up), masked_down(masks, down_w)
        grad = slots_side_by_side(got_ref, group, slots, rows)
        grad_hidden = dot(grad, w_down, (1, 1))
        both = jnp.concatenate([grad_hidden * dgate_ref[group], grad_hidden * dup_ref[group]], axis=1).astype(bf16)
        back = dot(both, w_in, (1, 1))
        store_slots(out_ref, back.astype(bf16), group, slots, rows)
        picked = slots_side_by_side(picked_ref, group, slots, rows)
        ins = dot(picked, both, (0, 0))
        down = dot(hidden_ref[group], grad, (0, 0))
        target = (own_grad_ref, other_grad_ref)[group]
        for slot in range(slots):
            first, second = masks[slot]
            line = ins[block_cols(slot)]
            lane = down[:, block_cols(slot)]
            target[0, slot] = (line[:, block_cols(0)] * first + line[:, block_cols(1)] * second).astype(target.dtype)
            target[1, slot] = (line[:, block_cols(2)] * first + line[:, block_cols(3)] * second).astype(target.dtype)
            target[2, slot] = (lane[block_cols(0)] * first + lane[block_cols(1)] * second).astype(target.dtype)
        part = jnp.sum(picked.astype(f32) * back, axis=0, keepdims=True)
        parts.extend(part[:, block_cols(slot)] for slot in range(slots))
    aside = jnp.sum(got_ref[:, 2 * slots * rows :, :].astype(f32), axis=0)
    parts.append(aside[0:1])
    row_id = lax.broadcasted_iota(jnp.int32, (ASIDE, B), 0)
    sent = jnp.zeros((ASIDE, B), f32)
    for index, part in enumerate(parts):
        sent = jnp.where(row_id == index, part, sent)
    out_ref[:, 2 * slots * rows :, :] = jnp.broadcast_to(sent.astype(bf16)[None], (peers, ASIDE, B))


def last(
    slots,
    place_ref,
    got_ref,
    acts_ref,
    cot_ref,
    gains_ref,
    grad_ref,
    gain_ref,
    total_ref,
    *more_refs,
):
    peers = got_ref.shape[0]
    rows, width = acts_ref.shape
    half = lax.axis_index("za")
    gain_refs = more_refs[-SUMS:]
    sum_blocks(place_ref, got_ref, (total_ref, *more_refs[:-SUMS]), half, peers, slots)
    for gain_total_ref in gain_refs:
        gain_total_ref[...] = jnp.zeros_like(gain_total_ref)
    for peer in range(peers):
        aside = got_ref[peer, 2 * slots * rows :, :].astype(f32)
        for group in range(2):
            for slot in range(slots):
                place = slot_place(place_ref, half, peer, group, slot, peers, slots)
                row = feature_block(place)
                at = group * slots + slot
                gain_total_ref = gain_refs[at % SUMS]
                gain_total_ref[row] = gain_total_ref[row] + aside[at : at + 1]
        gain_ref[1:2, block_cols(peer)] = aside[2 * slots : 2 * slots + 1]
    inputs = acts_ref[...].astype(f32)
    scale_in = inverse_norm(jnp.sum(inputs * inputs, axis=1, keepdims=True), width)
    mixed = jnp.zeros((rows, B), f32)
    for block in range(width // B):
        cols = block_cols(block)
        normed_in = acts_ref[:, cols].astype(f32) * scale_in
        gain = gains_ref[0, 0:1, cols]
        mixed = mixed + total_ref[block] * gain * normed_in
        gain_ref[0:1, cols] = sum(ref[block] for ref in gain_refs) / gain
    mean = jnp.sum(mixed, axis=1, keepdims=True) / width
    for block in range(width // B):
        cols = block_cols(block)
        normed_in = acts_ref[:, cols].astype(f32) * scale_in
        scaled_in = total_ref[block] * gains_ref[0, 0:1, cols]
        grad = cot_ref[:, cols].astype(f32)
        grad_ref[:, cols] = (grad + scale_in * (scaled_in - normed_in * mean)).astype(bf16)


def finish(own_ref, other_ref, gain_ref, gain_other_ref, gate_ref, up_ref, down_ref, gain_out):
    for kind, target in enumerate((gate_ref, up_ref, down_ref)):
        target[0] = (own_ref[kind] + other_ref[kind].astype(f32)).astype(bf16)
    gain_out[0] = gain_ref[...] + gain_other_ref[...]


def call(kernel, name, outs, operands, scratch=(), far_in=(), far_out=()):
    near, far = pl.BlockSpec(memory_space=pltpu.VMEM), pl.BlockSpec(memory_space=pl.ANY)
    scalars = pl.BlockSpec(memory_space=pltpu.SMEM)
    specs = [
        far if index in far_in else scalars if value.dtype == jnp.int32 else near
        for index, value in enumerate(operands)
    ]
    return pl.pallas_call(
        kernel,
        name=name,
        out_shape=[jax.ShapeDtypeStruct(shape, dtype) for shape, dtype in outs],
        in_specs=specs,
        out_specs=[far if index in far_out else near for index in range(len(outs))],
        scratch_shapes=list(scratch),
        compiler_params=pltpu.CompilerParams(vmem_limit_bytes=40 * 1024 * 1024),
    )(*operands)


def body(acts, cotangent, gains, gate_blocks, up_blocks, down_blocks, block_place):
    rows, width = acts.shape
    slots = gate_blocks.shape[1]
    peer_axes = ("zb", "xc")
    peers = lax.axis_size(peer_axes)
    features = width // B
    sent_rows = 2 * slots * rows
    tokens = peers * rows

    def to_other(value):
        return lax.ppermute(value, "za", [(0, 1), (1, 0)])

    def exchange(value):
        return lax.all_to_all(value, peer_axes, split_axis=0, concat_axis=0, tiled=True)

    feature_sums = pltpu.VMEM((features, rows, B), f32)
    feature_blocks = pltpu.VMEM((features, rows, B), bf16)

    own = (gate_blocks, up_blocks, down_blocks)
    both = (*own, *(to_other(value) for value in own))
    (sent,) = call(
        functools.partial(send_normed, slots),
        "send_normed",
        [((peers, sent_rows, B), bf16)],
        (block_place, acts, gains),
        [feature_blocks],
    )
    picked = exchange(sent)
    hidden, dgate, dup = call(
        gates,
        "gates",
        [((2, tokens, 2 * B), bf16), ((2, tokens, 2 * B), f32), ((2, tokens, 2 * B), f32)],
        (block_place, picked, both[0], both[1], both[3], both[4]),
    )
    (terms,) = call(
        down_terms,
        "down_terms",
        [((peers, sent_rows, B), bf16)],
        (block_place, hidden, both[2], both[5]),
    )
    layer_out, grad_sent = call(
        functools.partial(middle, slots),
        "middle",
        [((rows, width), bf16), ((peers, sent_rows + ASIDE, B), bf16)],
        (block_place, exchange(terms), acts, cotangent, gains),
        [feature_blocks] + [feature_sums] * SUMS,
    )
    weights = (3, slots, B, B)
    back_sent, own_grads, other_grads = call(
        backward,
        "backward",
        [((peers, sent_rows + ASIDE, B), bf16), (weights, f32), (weights, bf16)],
        (block_place, exchange(grad_sent), picked, *both, hidden, dgate, dup),
    )
    grads_got = to_other(other_grads)
    input_grad, gain_half = call(
        functools.partial(last, slots),
        "last",
        [((rows, width), bf16), ((2, width), f32)],
        (block_place, exchange(back_sent), acts, cotangent, gains),
        [feature_sums] * SUMS + [pltpu.VMEM((features, 1, B), f32)] * SUMS,
    )
    section = ("y", "zh")
    count = lax.axis_size(section)
    grad_back = lax.ppermute(input_grad, section, [(source, source - 1) for source in range(1, count)])
    gain_other = to_other(gain_half)
    gate_grad, up_grad, down_grad, gain_grad = call(
        finish,
        "finish",
        [((1, slots, B, B), bf16)] * 3 + [((1, 2, width), f32)],
        (own_grads, grads_got, gain_half, gain_other),
    )
    return (layer_out, grad_back, gate_grad, up_grad, down_grad, gain_grad)


def solution(mesh):
    names = ("y", "zh", "za", "zb", "xc")
    split = Mesh(mesh.devices.reshape(4, 2, 2, 4, 8), names)
    section, tp = names[:2], names[2:]
    tokens = P(names, None)
    blocks = P(section, tp, None, None)
    whole = P(section, None, None)
    return jax.shard_map(
        body,
        mesh=split,
        in_specs=(tokens, tokens, whole, blocks, blocks, blocks, P(section, None)),
        out_specs=(tokens, tokens, blocks, blocks, blocks, whole),
        check_vma=False,
    )
```

```python
import functools

import jax
import jax.numpy as jnp
from jax import lax
from jax.experimental import pallas as pl
from jax.experimental.pallas import tpu as pltpu
from jax.sharding import Mesh
from jax.sharding import PartitionSpec as P

epsilon = 1e-05
f32 = jnp.float32
bf16 = jnp.bfloat16
B = 128
SUMS = 3
ASIDE = 8


def dot(left, right, contract):
    return lax.dot_general(left, right, ((contract[:1], contract[1:]), ((), ())), preferred_element_type=f32)


def block_cols(index):
    return slice(index * B, (index + 1) * B)


def slot_rows(index, rows):
    return slice(index * rows, (index + 1) * rows)


def slots_side_by_side(got_ref, group, slots, rows):
    parts = [got_ref[:, slot_rows(group * slots + slot, rows), :] for slot in range(slots)]
    return jnp.concatenate([part.reshape(-1, B) for part in parts], axis=1)


def store_slots(out_ref, values, group, slots, rows):
    for slot in range(slots):
        out_ref[:, slot_rows(group * slots + slot, rows), :] = values[:, block_cols(slot)].reshape(-1, rows, B)


def slot_place(place_ref, half, peer, group, slot, peers, slots):
    zs = lax.axis_size("zb")
    device = peer % zs * (peers // zs) + peer // zs
    return place_ref[0, ((half ^ group) * peers + device) * slots + slot]


def feature_block(place):
    return lax.shift_right_logical(jnp.maximum(place, 0), 1)


def column_masks(place):
    live = place >= 0
    odd = (place & 1) == 1
    first = jnp.where(live & jnp.logical_not(odd), 1.0, 0.0).astype(f32)
    second = jnp.where(live & odd, 1.0, 0.0).astype(f32)
    return first, second


def scaled_block(block, factor):
    return block * jnp.full(block.shape, factor, f32).astype(bf16)


def pick_blocks(place_ref, blocks_ref, out_ref, half, peers, slots):
    rows = blocks_ref.shape[1]
    for peer in range(peers):
        for group in range(2):
            for slot in range(slots):
                place = slot_place(place_ref, half, peer, group, slot, peers, slots)
                out_ref[peer, slot_rows(group * slots + slot, rows), :] = blocks_ref[feature_block(place)]


def sum_blocks(place_ref, got_ref, total_refs, half, peers, slots):
    for total_ref in total_refs:
        total_ref[...] = jnp.zeros_like(total_ref)
    rows = total_refs[0].shape[1]
    count = 0
    for peer in range(peers):
        for group in range(2):
            for slot in range(slots):
                place = slot_place(place_ref, half, peer, group, slot, peers, slots)
                row = feature_block(place)
                total_ref = total_refs[count % len(total_refs)]
                count += 1
                term = got_ref[peer, slot_rows(group * slots + slot, rows), :].astype(f32)
                total_ref[row] = total_ref[row] + term
    for total_ref in total_refs[1:]:
        total_refs[0][...] += total_ref[...]


def inverse_norm(squares, width):
    return lax.rsqrt(squares / width + epsilon)


def send_normed(
    slots, place_ref, acts_ref, gains_ref, out_ref, blocks_ref
):
    peers = out_ref.shape[0]
    half = lax.axis_index("za")
    inputs = acts_ref[...].astype(f32)
    scale_in = inverse_norm(jnp.sum(inputs * inputs, axis=1, keepdims=True), inputs.shape[1])
    normed = (inputs * scale_in * gains_ref[0, 0:1, :]).astype(bf16)
    for row in range(blocks_ref.shape[0]):
        blocks_ref[row] = normed[:, block_cols(row)]
    pick_blocks(place_ref, blocks_ref, out_ref, half, peers, slots)


def own_peer():
    return lax.axis_index("xc") * lax.axis_size("zb") + lax.axis_index("zb")


def slot_masks(place_ref, half, peer, group, peers, slots):
    return [
        column_masks(slot_place(place_ref, half, peer, group, slot, peers, slots)) for slot in range(slots)
    ]


def masked_in(masks, gate_ref, up_ref):
    lines = []
    for slot, (first, second) in enumerate(masks):
        gate, up = gate_ref[0, slot], up_ref[0, slot]
        parts = [scaled_block(block, mask) for block in (gate, up) for mask in (first, second)]
        lines.append(jnp.concatenate(parts, axis=1))
    return jnp.concatenate(lines, axis=0)


def masked_down(masks, down_ref):
    parts = []
    for slot, (first, second) in enumerate(masks):
        down = down_ref[0, slot]
        parts.append(jnp.concatenate([scaled_block(down, first), scaled_block(down, second)], axis=0))
    return jnp.concatenate(parts, axis=1)


def gates(place_ref, got_ref, gate0, up0, gate1, up1, hidden_ref, dgate_ref, dup_ref):
    peers = got_ref.shape[0]
    slots = gate0.shape[1]
    rows = got_ref.shape[1] // (2 * slots)
    half, peer = lax.axis_index("za"), own_peer()
    for group, (gate, up) in enumerate(((gate0, up0), (gate1, up1))):
        masks = slot_masks(place_ref, half, peer, group, peers, slots)
        picked = slots_side_by_side(got_ref, group, slots, rows)
        sums = dot(picked, masked_in(masks, gate, up), (1, 0))
        gate_sum, up_sum = sums[:, : 2 * B], sums[:, 2 * B :]
        sigmoid = jax.nn.sigmoid(gate_sum)
        silu = gate_sum * sigmoid
        hidden_ref[group] = (silu * up_sum).astype(bf16)
        dgate_ref[group] = up_sum * sigmoid * (1.0 + gate_sum * (1.0 - sigmoid))
        dup_ref[group] = silu


def down_terms(place_ref, hidden_ref, down0, down1, terms_ref):
    peers = terms_ref.shape[0]
    slots = down0.shape[1]
    rows = terms_ref.shape[1] // (2 * slots)
    half, peer = lax.axis_index("za"), own_peer()
    for group, down in enumerate((down0, down1)):
        masks = slot_masks(place_ref, half, peer, group, peers, slots)
        terms = dot(hidden_ref[group], masked_down(masks, down), (1, 0)).astype(bf16)
        store_slots(terms_ref, terms, group, slots, rows)


def middle(
    slots,
    place_ref,
    got_ref,
    acts_ref,
    cot_ref,
    gains_ref,
    layer_ref,
    out_ref,
    blocks_ref,
    total_ref,
    *more_refs,
):
    peers = got_ref.shape[0]
    rows, width = acts_ref.shape
    half = lax.axis_index("za")
    sum_blocks(place_ref, got_ref, (total_ref, *more_refs), half, peers, slots)
    branch = total_ref[...]
    squares = jnp.sum(jnp.sum(branch * branch, axis=0), axis=1, keepdims=True)
    scale_out = inverse_norm(squares, width)
    row_id = lax.broadcasted_iota(jnp.int32, (ASIDE, B), 0)
    mixed = jnp.zeros((rows, B), f32)
    for block in range(width // B):
        cols = block_cols(block)
        grad = cot_ref[:, cols].astype(f32)
        unit = total_ref[block] * scale_out
        gain = gains_ref[0, 1:2, cols]
        layer_ref[:, cols] = (acts_ref[:, cols].astype(f32) + unit * gain).astype(bf16)
        mixed = mixed + grad * gain * unit
        part = jnp.sum(grad * unit, axis=0, keepdims=True)
        out_ref[block, 2 * slots * rows :, :] = jnp.where(row_id == 0, part, 0.0).astype(bf16)
    mean = jnp.sum(mixed, axis=1, keepdims=True) / width
    for block in range(width // B):
        cols = block_cols(block)
        scaled = cot_ref[:, cols].astype(f32) * gains_ref[0, 1:2, cols]
        unit = total_ref[block] * scale_out
        blocks_ref[block] = (scale_out * (scaled - unit * mean)).astype(bf16)
    pick_blocks(place_ref, blocks_ref, out_ref, half, peers, slots)


def backward(
    place_ref,
    got_ref,
    picked_ref,
    gate0,
    up0,
    down0,
    gate1,
    up1,
    down1,
    hidden_ref,
    dgate_ref,
    dup_ref,
    out_ref,
    own_grad_ref,
    other_grad_ref,
):
    peers = got_ref.shape[0]
    slots = gate0.shape[1]
    rows = picked_ref.shape[1] // (2 * slots)
    half, peer = lax.axis_index("za"), own_peer()
    parts = []
    for group, (gate, up, down_w) in enumerate(((gate0, up0, down0), (gate1, up1, down1))):
        masks = slot_masks(place_ref, half, peer, group, peers, slots)
        w_in, w_down = masked_in(masks, gate, up), masked_down(masks, down_w)
        grad = slots_side_by_side(got_ref, group, slots, rows)
        grad_hidden = dot(grad, w_down, (1, 1))
        both = jnp.concatenate([grad_hidden * dgate_ref[group], grad_hidden * dup_ref[group]], axis=1).astype(bf16)
        back = dot(both, w_in, (1, 1))
        store_slots(out_ref, back.astype(bf16), group, slots, rows)
        picked = slots_side_by_side(picked_ref, group, slots, rows)
        ins = dot(picked, both, (0, 0))
        down = dot(hidden_ref[group], grad, (0, 0))
        target = (own_grad_ref, other_grad_ref)[group]
        for slot in range(slots):
            first, second = masks[slot]
            line = ins[block_cols(slot)]
            lane = down[:, block_cols(slot)]
            target[0, slot] = (line[:, block_cols(0)] * first + line[:, block_cols(1)] * second).astype(target.dtype)
            target[1, slot] = (line[:, block_cols(2)] * first + line[:, block_cols(3)] * second).astype(target.dtype)
            target[2, slot] = (lane[block_cols(0)] * first + lane[block_cols(1)] * second).astype(target.dtype)
        part = jnp.sum(picked.astype(f32) * back, axis=0, keepdims=True)
        parts.extend(part[:, block_cols(slot)] for slot in range(slots))
    aside = jnp.sum(got_ref[:, 2 * slots * rows :, :].astype(f32), axis=0)
    parts.append(aside[0:1])
    row_id = lax.broadcasted_iota(jnp.int32, (ASIDE, B), 0)
    sent = jnp.zeros((ASIDE, B), f32)
    for index, part in enumerate(parts):
        sent = jnp.where(row_id == index, part, sent)
    out_ref[:, 2 * slots * rows :, :] = jnp.broadcast_to(sent.astype(bf16)[None], (peers, ASIDE, B))


def last(
    slots,
    place_ref,
    got_ref,
    acts_ref,
    cot_ref,
    gains_ref,
    grad_ref,
    gain_out,
    gain_ref,
    total_ref,
    *more_refs,
):
    peers = got_ref.shape[0]
    rows, width = acts_ref.shape
    half = lax.axis_index("za")
    gain_refs = more_refs[-SUMS:]
    sum_blocks(place_ref, got_ref, (total_ref, *more_refs[:-SUMS]), half, peers, slots)
    for gain_total_ref in gain_refs:
        gain_total_ref[...] = jnp.zeros_like(gain_total_ref)
    for peer in range(peers):
        aside = got_ref[peer, 2 * slots * rows :, :].astype(f32)
        for group in range(2):
            for slot in range(slots):
                place = slot_place(place_ref, half, peer, group, slot, peers, slots)
                row = feature_block(place)
                at = group * slots + slot
                gain_total_ref = gain_refs[at % SUMS]
                gain_total_ref[row] = gain_total_ref[row] + aside[at : at + 1]
        gain_ref[1:2, block_cols(peer)] = aside[2 * slots : 2 * slots + 1]
    inputs = acts_ref[...].astype(f32)
    scale_in = inverse_norm(jnp.sum(inputs * inputs, axis=1, keepdims=True), width)
    mixed = jnp.zeros((rows, B), f32)
    for block in range(width // B):
        cols = block_cols(block)
        normed_in = acts_ref[:, cols].astype(f32) * scale_in
        gain = gains_ref[0, 0:1, cols]
        mixed = mixed + total_ref[block] * gain * normed_in
        gain_ref[0:1, cols] = sum(ref[block] for ref in gain_refs) / gain
    gain_out[...] = gain_ref[...].astype(bf16)
    mean = jnp.sum(mixed, axis=1, keepdims=True) / width
    for block in range(width // B):
        cols = block_cols(block)
        normed_in = acts_ref[:, cols].astype(f32) * scale_in
        scaled_in = total_ref[block] * gains_ref[0, 0:1, cols]
        grad = cot_ref[:, cols].astype(f32)
        grad_ref[:, cols] = (grad + scale_in * (scaled_in - normed_in * mean)).astype(bf16)


def finish(own_ref, other_ref, gain_ref, gain_other_ref, input_ref, gate_ref, up_ref, down_ref, gain_out, back_ref):
    for kind, target in enumerate((gate_ref, up_ref, down_ref)):
        target[0] = (own_ref[kind] + other_ref[kind].astype(f32)).astype(bf16)
    gain_out[0] = gain_ref[...].astype(f32) + gain_other_ref[...].astype(f32)
    back_ref[...] = input_ref[...]


def call(kernel, name, outs, operands, scratch=(), far_in=(), far_out=()):
    near, far = pl.BlockSpec(memory_space=pltpu.VMEM), pl.BlockSpec(memory_space=pl.ANY)
    scalars = pl.BlockSpec(memory_space=pltpu.SMEM)
    specs = [
        far if index in far_in else scalars if value.dtype == jnp.int32 else near
        for index, value in enumerate(operands)
    ]
    return pl.pallas_call(
        kernel,
        name=name,
        out_shape=[jax.ShapeDtypeStruct(shape, dtype) for shape, dtype in outs],
        in_specs=specs,
        out_specs=[far if index in far_out else near for index in range(len(outs))],
        scratch_shapes=list(scratch),
        compiler_params=pltpu.CompilerParams(vmem_limit_bytes=40 * 1024 * 1024),
    )(*operands)


def body(acts, cotangent, gains, gate_blocks, up_blocks, down_blocks, block_place):
    rows, width = acts.shape
    slots = gate_blocks.shape[1]
    peer_axes = ("xc", "zb")
    peers = lax.axis_size(peer_axes)
    features = width // B
    sent_rows = 2 * slots * rows
    tokens = peers * rows

    def to_other(value):
        return lax.ppermute(value, "za", [(0, 1), (1, 0)])

    def exchange(value):
        return lax.all_to_all(value, peer_axes, split_axis=0, concat_axis=0, tiled=True)

    feature_sums = pltpu.VMEM((features, rows, B), f32)
    feature_blocks = pltpu.VMEM((features, rows, B), bf16)

    own = (gate_blocks, up_blocks, down_blocks)
    both = (*own, *(to_other(value) for value in own))
    (sent,) = call(
        functools.partial(send_normed, slots),
        "send_normed",
        [((peers, sent_rows, B), bf16)],
        (block_place, acts, gains),
        [feature_blocks],
    )
    picked = exchange(sent)
    hidden, dgate, dup = call(
        gates,
        "gates",
        [((2, tokens, 2 * B), bf16), ((2, tokens, 2 * B), f32), ((2, tokens, 2 * B), f32)],
        (block_place, picked, both[0], both[1], both[3], both[4]),
    )
    (terms,) = call(
        down_terms,
        "down_terms",
        [((peers, sent_rows, B), bf16)],
        (block_place, hidden, both[2], both[5]),
    )
    layer_out, grad_sent = call(
        functools.partial(middle, slots),
        "middle",
        [((rows, width), bf16), ((peers, sent_rows + ASIDE, B), bf16)],
        (block_place, exchange(terms), acts, cotangent, gains),
        [feature_blocks] + [feature_sums] * SUMS,
    )
    weights = (3, slots, B, B)
    back_sent, own_grads, other_grads = call(
        backward,
        "backward",
        [((peers, sent_rows + ASIDE, B), bf16), (weights, f32), (weights, bf16)],
        (block_place, exchange(grad_sent), picked, *both, hidden, dgate, dup),
    )
    grads_got = to_other(other_grads)
    input_grad, gain_half = call(
        functools.partial(last, slots),
        "last",
        [((rows, width), bf16), ((2, width), bf16)],
        (block_place, exchange(back_sent), acts, cotangent, gains),
        [pltpu.VMEM((2, width), f32)] + [feature_sums] * SUMS + [pltpu.VMEM((features, 1, B), f32)] * SUMS,
    )
    section = ("y", "zh")
    count = lax.axis_size(section)
    grad_back = lax.ppermute(input_grad, section, [(source, source - 1) for source in range(1, count)])
    gain_other = to_other(gain_half)
    gate_grad, up_grad, down_grad, gain_grad, grad_back = call(
        finish,
        "finish",
        [((1, slots, B, B), bf16)] * 3 + [((1, 2, width), f32), ((rows, width), bf16)],
        (own_grads, grads_got, gain_half, gain_other, grad_back),
    )
    return (layer_out, grad_back, gate_grad, up_grad, down_grad, gain_grad)


def solution(mesh):
    names = ("y", "zh", "za", "zb", "xc")
    split = Mesh(mesh.devices.reshape(4, 2, 2, 4, 8), names)
    section, tp = names[:2], names[2:]
    tokens = P(names, None)
    blocks = P(section, tp, None, None)
    whole = P(section, None, None)
    return jax.shard_map(
        body,
        mesh=split,
        in_specs=(tokens, tokens, whole, blocks, blocks, blocks, P(section, None)),
        out_specs=(tokens, tokens, blocks, blocks, blocks, whole),
        check_vma=False,
    )
```

```python
import functools

import jax
import jax.numpy as jnp
from jax import lax
from jax.experimental import pallas as pl
from jax.experimental.pallas import tpu as pltpu
from jax.sharding import Mesh
from jax.sharding import PartitionSpec as P

epsilon = 1e-05
f32 = jnp.float32
bf16 = jnp.bfloat16
B = 128
SUMS = 3
ASIDE = 8


def dot(left, right, contract):
    return lax.dot_general(left, right, ((contract[:1], contract[1:]), ((), ())), preferred_element_type=f32)


def block_cols(index):
    return slice(index * B, (index + 1) * B)


def slot_rows(index, rows):
    return slice(index * rows, (index + 1) * rows)


def slots_side_by_side(got_ref, group, slots, rows):
    parts = [got_ref[:, slot_rows(group * slots + slot, rows), :] for slot in range(slots)]
    return jnp.concatenate([part.reshape(-1, B) for part in parts], axis=1)


def store_slots(out_ref, values, group, slots, rows):
    for slot in range(slots):
        out_ref[:, slot_rows(group * slots + slot, rows), :] = values[:, block_cols(slot)].reshape(-1, rows, B)


def slot_place(place_ref, half, peer, group, slot, peers, slots):
    device = peer % 4 * 8 + peer // 4 % 4 * 2 + peer // 16
    return place_ref[0, ((half ^ group) * peers + device) * slots + slot]


def feature_block(place):
    return lax.shift_right_logical(jnp.maximum(place, 0), 1)


def column_masks(place):
    live = place >= 0
    odd = (place & 1) == 1
    first = jnp.where(live & jnp.logical_not(odd), 1.0, 0.0).astype(f32)
    second = jnp.where(live & odd, 1.0, 0.0).astype(f32)
    return first, second


def scaled_block(block, factor):
    return block * jnp.full(block.shape, factor, f32).astype(bf16)


def pick_blocks(place_ref, blocks_ref, out_ref, half, peers, slots):
    rows = blocks_ref.shape[1]
    for peer in range(peers):
        for group in range(2):
            for slot in range(slots):
                place = slot_place(place_ref, half, peer, group, slot, peers, slots)
                out_ref[peer, slot_rows(group * slots + slot, rows), :] = blocks_ref[feature_block(place)]


def sum_blocks(place_ref, got_ref, total_refs, half, peers, slots):
    for total_ref in total_refs:
        total_ref[...] = jnp.zeros_like(total_ref)
    rows = total_refs[0].shape[1]
    count = 0
    for peer in range(peers):
        for group in range(2):
            for slot in range(slots):
                place = slot_place(place_ref, half, peer, group, slot, peers, slots)
                row = feature_block(place)
                total_ref = total_refs[count % len(total_refs)]
                count += 1
                term = got_ref[peer, slot_rows(group * slots + slot, rows), :].astype(f32)
                total_ref[row] = total_ref[row] + term
    for total_ref in total_refs[1:]:
        total_refs[0][...] += total_ref[...]


def inverse_norm(squares, width):
    return lax.rsqrt(squares / width + epsilon)


def send_normed(
    slots, place_ref, acts_ref, gains_ref, out_ref, blocks_ref
):
    peers = out_ref.shape[0]
    half = lax.axis_index("za")
    inputs = acts_ref[...].astype(f32)
    scale_in = inverse_norm(jnp.sum(inputs * inputs, axis=1, keepdims=True), inputs.shape[1])
    normed = (inputs * scale_in * gains_ref[0, 0:1, :]).astype(bf16)
    for row in range(blocks_ref.shape[0]):
        blocks_ref[row] = normed[:, block_cols(row)]
    pick_blocks(place_ref, blocks_ref, out_ref, half, peers, slots)


def own_peer():
    return (lax.axis_index("c") * 4 + lax.axis_index("x")) * 4 + lax.axis_index("zb")


def slot_masks(place_ref, half, peer, group, peers, slots):
    return [
        column_masks(slot_place(place_ref, half, peer, group, slot, peers, slots)) for slot in range(slots)
    ]


def masked_in(masks, gate_ref, up_ref):
    lines = []
    for slot, (first, second) in enumerate(masks):
        gate, up = gate_ref[0, slot], up_ref[0, slot]
        parts = [scaled_block(block, mask) for block in (gate, up) for mask in (first, second)]
        lines.append(jnp.concatenate(parts, axis=1))
    return jnp.concatenate(lines, axis=0)


def masked_down(masks, down_ref):
    parts = []
    for slot, (first, second) in enumerate(masks):
        down = down_ref[0, slot]
        parts.append(jnp.concatenate([scaled_block(down, first), scaled_block(down, second)], axis=0))
    return jnp.concatenate(parts, axis=1)


def gates(place_ref, got_ref, gate0, up0, gate1, up1, hidden_ref, dgate_ref, dup_ref):
    peers = got_ref.shape[0]
    slots = gate0.shape[1]
    rows = got_ref.shape[1] // (2 * slots)
    half, peer = lax.axis_index("za"), own_peer()
    for group, (gate, up) in enumerate(((gate0, up0), (gate1, up1))):
        masks = slot_masks(place_ref, half, peer, group, peers, slots)
        picked = slots_side_by_side(got_ref, group, slots, rows)
        sums = dot(picked, masked_in(masks, gate, up), (1, 0))
        gate_sum, up_sum = sums[:, : 2 * B], sums[:, 2 * B :]
        sigmoid = jax.nn.sigmoid(gate_sum)
        silu = gate_sum * sigmoid
        hidden_ref[group] = (silu * up_sum).astype(bf16)
        dgate_ref[group] = up_sum * sigmoid * (1.0 + gate_sum * (1.0 - sigmoid))
        dup_ref[group] = silu


def down_terms(place_ref, hidden_ref, down0, down1, terms_ref):
    peers = terms_ref.shape[0]
    slots = down0.shape[1]
    rows = terms_ref.shape[1] // (2 * slots)
    half, peer = lax.axis_index("za"), own_peer()
    for group, down in enumerate((down0, down1)):
        masks = slot_masks(place_ref, half, peer, group, peers, slots)
        terms = dot(hidden_ref[group], masked_down(masks, down), (1, 0)).astype(bf16)
        store_slots(terms_ref, terms, group, slots, rows)


def middle(
    slots,
    place_ref,
    got_ref,
    acts_ref,
    cot_ref,
    gains_ref,
    layer_ref,
    out_ref,
    blocks_ref,
    total_ref,
    *more_refs,
):
    peers = got_ref.shape[0]
    rows, width = acts_ref.shape
    half = lax.axis_index("za")
    sum_blocks(place_ref, got_ref, (total_ref, *more_refs), half, peers, slots)
    branch = total_ref[...]
    squares = jnp.sum(jnp.sum(branch * branch, axis=0), axis=1, keepdims=True)
    scale_out = inverse_norm(squares, width)
    row_id = lax.broadcasted_iota(jnp.int32, (ASIDE, B), 0)
    mixed = jnp.zeros((rows, B), f32)
    for block in range(width // B):
        cols = block_cols(block)
        grad = cot_ref[:, cols].astype(f32)
        unit = total_ref[block] * scale_out
        gain = gains_ref[0, 1:2, cols]
        layer_ref[:, cols] = (acts_ref[:, cols].astype(f32) + unit * gain).astype(bf16)
        mixed = mixed + grad * gain * unit
        part = jnp.sum(grad * unit, axis=0, keepdims=True)
        out_ref[block, 2 * slots * rows :, :] = jnp.where(row_id == 0, part, 0.0).astype(bf16)
    mean = jnp.sum(mixed, axis=1, keepdims=True) / width
    for block in range(width // B):
        cols = block_cols(block)
        scaled = cot_ref[:, cols].astype(f32) * gains_ref[0, 1:2, cols]
        unit = total_ref[block] * scale_out
        blocks_ref[block] = (scale_out * (scaled - unit * mean)).astype(bf16)
    pick_blocks(place_ref, blocks_ref, out_ref, half, peers, slots)


def backward(
    place_ref,
    got_ref,
    picked_ref,
    gate0,
    up0,
    down0,
    gate1,
    up1,
    down1,
    hidden_ref,
    dgate_ref,
    dup_ref,
    out_ref,
    own_grad_ref,
    other_grad_ref,
):
    peers = got_ref.shape[0]
    slots = gate0.shape[1]
    rows = picked_ref.shape[1] // (2 * slots)
    half, peer = lax.axis_index("za"), own_peer()
    parts = []
    for group, (gate, up, down_w) in enumerate(((gate0, up0, down0), (gate1, up1, down1))):
        masks = slot_masks(place_ref, half, peer, group, peers, slots)
        w_in, w_down = masked_in(masks, gate, up), masked_down(masks, down_w)
        grad = slots_side_by_side(got_ref, group, slots, rows)
        grad_hidden = dot(grad, w_down, (1, 1))
        both = jnp.concatenate([grad_hidden * dgate_ref[group], grad_hidden * dup_ref[group]], axis=1).astype(bf16)
        back = dot(both, w_in, (1, 1))
        store_slots(out_ref, back.astype(bf16), group, slots, rows)
        picked = slots_side_by_side(picked_ref, group, slots, rows)
        ins = dot(picked, both, (0, 0))
        down = dot(hidden_ref[group], grad, (0, 0))
        target = (own_grad_ref, other_grad_ref)[group]
        for slot in range(slots):
            first, second = masks[slot]
            line = ins[block_cols(slot)]
            lane = down[:, block_cols(slot)]
            target[0, slot] = (line[:, block_cols(0)] * first + line[:, block_cols(1)] * second).astype(target.dtype)
            target[1, slot] = (line[:, block_cols(2)] * first + line[:, block_cols(3)] * second).astype(target.dtype)
            target[2, slot] = (lane[block_cols(0)] * first + lane[block_cols(1)] * second).astype(target.dtype)
        part = jnp.sum(picked.astype(f32) * back, axis=0, keepdims=True)
        parts.extend(part[:, block_cols(slot)] for slot in range(slots))
    aside = jnp.sum(got_ref[:, 2 * slots * rows :, :].astype(f32), axis=0)
    parts.append(aside[0:1])
    row_id = lax.broadcasted_iota(jnp.int32, (ASIDE, B), 0)
    sent = jnp.zeros((ASIDE, B), f32)
    for index, part in enumerate(parts):
        sent = jnp.where(row_id == index, part, sent)
    out_ref[:, 2 * slots * rows :, :] = jnp.broadcast_to(sent.astype(bf16)[None], (peers, ASIDE, B))


def last(
    slots,
    place_ref,
    got_ref,
    acts_ref,
    cot_ref,
    gains_ref,
    grad_ref,
    gain_out,
    gain_ref,
    total_ref,
    *more_refs,
):
    peers = got_ref.shape[0]
    rows, width = acts_ref.shape
    half = lax.axis_index("za")
    gain_refs = more_refs[-SUMS:]
    sum_blocks(place_ref, got_ref, (total_ref, *more_refs[:-SUMS]), half, peers, slots)
    for gain_total_ref in gain_refs:
        gain_total_ref[...] = jnp.zeros_like(gain_total_ref)
    for peer in range(peers):
        aside = got_ref[peer, 2 * slots * rows :, :].astype(f32)
        for group in range(2):
            for slot in range(slots):
                place = slot_place(place_ref, half, peer, group, slot, peers, slots)
                row = feature_block(place)
                at = group * slots + slot
                gain_total_ref = gain_refs[at % SUMS]
                gain_total_ref[row] = gain_total_ref[row] + aside[at : at + 1]
        gain_ref[1:2, block_cols(peer)] = aside[2 * slots : 2 * slots + 1]
    inputs = acts_ref[...].astype(f32)
    scale_in = inverse_norm(jnp.sum(inputs * inputs, axis=1, keepdims=True), width)
    mixed = jnp.zeros((rows, B), f32)
    for block in range(width // B):
        cols = block_cols(block)
        normed_in = acts_ref[:, cols].astype(f32) * scale_in
        gain = gains_ref[0, 0:1, cols]
        mixed = mixed + total_ref[block] * gain * normed_in
        gain_ref[0:1, cols] = sum(ref[block] for ref in gain_refs) / gain
    gain_out[...] = gain_ref[...].astype(bf16)
    mean = jnp.sum(mixed, axis=1, keepdims=True) / width
    for block in range(width // B):
        cols = block_cols(block)
        normed_in = acts_ref[:, cols].astype(f32) * scale_in
        scaled_in = total_ref[block] * gains_ref[0, 0:1, cols]
        grad = cot_ref[:, cols].astype(f32)
        grad_ref[:, cols] = (grad + scale_in * (scaled_in - normed_in * mean)).astype(bf16)


def finish(own_ref, other_ref, gain_ref, gain_other_ref, input_ref, gate_ref, up_ref, down_ref, gain_out, back_ref):
    for kind, target in enumerate((gate_ref, up_ref, down_ref)):
        target[0] = (own_ref[kind] + other_ref[kind].astype(f32)).astype(bf16)
    gain_out[0] = gain_ref[...].astype(f32) + gain_other_ref[...].astype(f32)
    back_ref[...] = input_ref[...]


def call(kernel, name, outs, operands, scratch=(), far_in=(), far_out=()):
    near, far = pl.BlockSpec(memory_space=pltpu.VMEM), pl.BlockSpec(memory_space=pl.ANY)
    scalars = pl.BlockSpec(memory_space=pltpu.SMEM)
    specs = [
        far if index in far_in else scalars if value.dtype == jnp.int32 else near
        for index, value in enumerate(operands)
    ]
    return pl.pallas_call(
        kernel,
        name=name,
        out_shape=[jax.ShapeDtypeStruct(shape, dtype) for shape, dtype in outs],
        in_specs=specs,
        out_specs=[far if index in far_out else near for index in range(len(outs))],
        scratch_shapes=list(scratch),
        compiler_params=pltpu.CompilerParams(vmem_limit_bytes=40 * 1024 * 1024),
    )(*operands)


def body(acts, cotangent, gains, gate_blocks, up_blocks, down_blocks, block_place):
    rows, width = acts.shape
    slots = gate_blocks.shape[1]
    peer_axes = ("c", "x", "zb")
    peers = lax.axis_size(peer_axes)
    features = width // B
    sent_rows = 2 * slots * rows
    tokens = peers * rows

    def to_other(value):
        return lax.ppermute(value, "za", [(0, 1), (1, 0)])

    def exchange(value):
        return lax.all_to_all(value, peer_axes, split_axis=0, concat_axis=0, tiled=True)

    feature_sums = pltpu.VMEM((features, rows, B), f32)
    feature_blocks = pltpu.VMEM((features, rows, B), bf16)

    own = (gate_blocks, up_blocks, down_blocks)
    both = (*own, *(to_other(value) for value in own))
    (sent,) = call(
        functools.partial(send_normed, slots),
        "send_normed",
        [((peers, sent_rows, B), bf16)],
        (block_place, acts, gains),
        [feature_blocks],
    )
    picked = exchange(sent)
    hidden, dgate, dup = call(
        gates,
        "gates",
        [((2, tokens, 2 * B), bf16), ((2, tokens, 2 * B), f32), ((2, tokens, 2 * B), f32)],
        (block_place, picked, both[0], both[1], both[3], both[4]),
    )
    (terms,) = call(
        down_terms,
        "down_terms",
        [((peers, sent_rows, B), bf16)],
        (block_place, hidden, both[2], both[5]),
    )
    layer_out, grad_sent = call(
        functools.partial(middle, slots),
        "middle",
        [((rows, width), bf16), ((peers, sent_rows + ASIDE, B), bf16)],
        (block_place, exchange(terms), acts, cotangent, gains),
        [feature_blocks] + [feature_sums] * SUMS,
    )
    weights = (3, slots, B, B)
    back_sent, own_grads, other_grads = call(
        backward,
        "backward",
        [((peers, sent_rows + ASIDE, B), bf16), (weights, f32), (weights, bf16)],
        (block_place, exchange(grad_sent), picked, *both, hidden, dgate, dup),
    )
    grads_got = to_other(other_grads)
    input_grad, gain_half = call(
        functools.partial(last, slots),
        "last",
        [((rows, width), bf16), ((2, width), bf16)],
        (block_place, exchange(back_sent), acts, cotangent, gains),
        [pltpu.VMEM((2, width), f32)] + [feature_sums] * SUMS + [pltpu.VMEM((features, 1, B), f32)] * SUMS,
    )
    section = ("y", "zh")
    count = lax.axis_size(section)
    grad_back = lax.ppermute(input_grad, section, [(source, source - 1) for source in range(1, count)])
    gain_other = to_other(gain_half)
    gate_grad, up_grad, down_grad, gain_grad, grad_back = call(
        finish,
        "finish",
        [((1, slots, B, B), bf16)] * 3 + [((1, 2, width), f32), ((rows, width), bf16)],
        (own_grads, grads_got, gain_half, gain_other, grad_back),
    )
    return (layer_out, grad_back, gate_grad, up_grad, down_grad, gain_grad)


def solution(mesh):
    names = ("y", "zh", "za", "zb", "x", "c")
    split = Mesh(mesh.devices.reshape(4, 2, 2, 4, 4, 2), names)
    section, tp = names[:2], names[2:]
    tokens = P(names, None)
    blocks = P(section, tp, None, None)
    whole = P(section, None, None)
    return jax.shard_map(
        body,
        mesh=split,
        in_specs=(tokens, tokens, whole, blocks, blocks, blocks, P(section, None)),
        out_specs=(tokens, tokens, blocks, blocks, blocks, whole),
        check_vma=False,
    )
```
